128 devices in a mesh: grp: 4 (over x), dev: 32 (over y, z, core).
Axes of the slice: x: 4, y: 4, z: 4, core: 2. Of those that a mesh axis runs over, the one named last changes fastest.
Arguments:
- positions: bfloat16 [3, 524288], P(None, ('grp', 'dev')), may hold values from 0 to 1.5
- features: bfloat16 [524288, 128], P(('grp', 'dev')), may hold values from -6 to 6
- tile_first: int32 [1024], P(('grp', 'dev')), may hold values from 0 to 31
- tile_second: int32 [1024], P(('grp', 'dev')), may hold values from 0 to 127
- count_first: int32 [1024], P(('grp', 'dev')), may hold values from 32 to 128
- count_second: int32 [1024], P(('grp', 'dev')), may hold values from 32 to 128
- w_first: bfloat16 [128, 128], replicated, may hold values from -0.5 to 0.5
- w_second: bfloat16 [128, 128], replicated, may hold values from -0.5 to 0.5
- radial_weight: bfloat16 [16, 128], replicated, may hold values from -3 to 3
- mix_weight: bfloat16 [128, 128], replicated, may hold values from -0.5 to 0.5
- out_weight: float32 [128], replicated, may hold values from -1.5 to 1.5
Outputs:
- forces: float32 [3, 524288], P(None, ('grp', 'dev'))
The draws below stay inside these ranges and needn't reach their ends.
All inputs are finite; a program needn't handle non-finite values.
Results may differ from the reference program's by a relative error of at most 0.0023.
Values may be sent and summed in bfloat16 or wider, within the bound.
A program may use at most 64 MiB of HBM per device.

```python
import jax
import jax.numpy as jnp
from jax import lax

CELL = 128
CELLS_DEV = 32
TILE_DEV = 8
LAT = 128
NB = 16
BEADS = 524288
TILES = 1024
N_GRP = 4
N_DEV = 32


def set_ends(drawn, key, low, high):
    shape = drawn.shape
    place = [jax.random.randint(jax.random.fold_in(key, axis), (), 0, shape[axis]) for axis in range(len(shape))]
    drawn = drawn.at[tuple(place)].set(low)
    longest = shape.index(max(shape))
    place[longest] = (place[longest] + 1) % shape[longest]
    return drawn.at[tuple(place)].set(high)


def steps_of(key, extent, cuts, least, top_value):
    level = 1.0
    for axis_at, blocks in cuts:
        draws = jax.random.uniform(jax.random.fold_in(jax.random.fold_in(key, 6), axis_at), (blocks,), jnp.float32, least / len(cuts), top_value / len(cuts))
        level = level * jnp.repeat(jnp.exp(draws), extent[axis_at] // blocks).reshape((-1,) + (1,) * (len(extent) - 1 - axis_at))
    return level


def bell_draw(key, dims, scale, bound, cuts=(), kind=jnp.bfloat16):
    factor_of = steps_of(key, dims, cuts, -0.22, 0.18) if cuts else 1.0
    result = jax.random.normal(key, dims, jnp.float32) * scale * factor_of
    return jnp.minimum(jnp.maximum(result, -bound), bound).astype(kind)


def setup_inputs(seed: int = 0) -> dict:
    arg_keys = jax.random.split(jax.random.key(seed), 12)
    return {
        "positions": jnp.clip(1.5 * jax.random.uniform(arg_keys[0], (3, BEADS), jnp.float32) ** steps_of(arg_keys[0], (3, BEADS), ((1, 128),), -0.2, 0.2), 0.0, 1.5).astype(jnp.bfloat16),
        "features": bell_draw(arg_keys[1], (BEADS, LAT), 1.0, 6.0, ((0, 128),)),
        "tile_first": set_ends(jax.random.randint(arg_keys[2], (TILES,), 0, CELLS_DEV), jax.random.fold_in(arg_keys[2], 1), 0, CELLS_DEV - 1).astype(jnp.int32),
        "tile_second": set_ends(jax.random.randint(arg_keys[3], (TILES,), 0, 4 * CELLS_DEV), jax.random.fold_in(arg_keys[3], 1), 0, (4 * CELLS_DEV) - 1).astype(jnp.int32),
        "count_first": set_ends(jax.random.randint(arg_keys[4], (TILES,), CELL // 4, CELL + 1), jax.random.fold_in(arg_keys[4], 1), CELL // 4, CELL).astype(jnp.int32),
        "count_second": set_ends(jax.random.randint(arg_keys[5], (TILES,), CELL // 4, CELL + 1), jax.random.fold_in(arg_keys[5], 1), CELL // 4, CELL).astype(jnp.int32),
        "w_first": bell_draw(arg_keys[6], (LAT, LAT), LAT ** -0.5, 0.5),
        "w_second": bell_draw(arg_keys[7], (LAT, LAT), LAT ** -0.5, 0.5),
        "radial_weight": bell_draw(arg_keys[8], (NB, LAT), 4 ** -0.5, 3.0),
        "mix_weight": bell_draw(arg_keys[9], (LAT, LAT), LAT ** -0.5, 0.5),
        "out_weight": bell_draw(arg_keys[10], (LAT,), (LAT // 8) ** -0.5, 1.5, (), jnp.float32),
    }


def project(features, weight):
    return jnp.dot(features, weight, preferred_element_type=jnp.float32).astype(jnp.bfloat16)


def silu_slope(values):
    sigma = jax.nn.sigmoid(values)
    return sigma * (1.0 + values * (1.0 - sigma))


def tile_gradients(first_pos, second_pos, first_proj, second_proj, first_live, second_live, radial_weight, mix_weight, out_weight):
    slots = first_pos.shape[1]
    diff = first_pos[:, :, None] - second_pos[:, None, :]
    dist_sq = jnp.sum(diff * diff, axis=0).reshape(-1)
    centers = jnp.arange(NB, dtype=jnp.float32) * (6.75 / NB)
    offset = dist_sq[None, :] - centers[:, None]
    basis_exact = jnp.exp(-2.0 * offset * offset)
    basis = basis_exact.astype(jnp.bfloat16)
    radial = lax.dot_general(basis, radial_weight, (((0,), (0,)), ((), ())), preferred_element_type=jnp.float32)
    radial = radial.reshape(slots, slots, -1)
    summed = radial + first_proj.astype(jnp.float32)[:, None, :] + second_proj.astype(jnp.float32)[None, :, :]
    summed = summed.reshape(slots * slots, -1)
    latent = jax.nn.silu(summed).astype(jnp.bfloat16)
    pre = jnp.dot(latent, mix_weight, preferred_element_type=jnp.float32)
    readout = jnp.sum(jax.nn.silu(pre) * out_weight[None, :], axis=1)
    weights = (first_live[:, None] * second_live[None, :]).reshape(-1) / slots
    envelope_base = 1.0 - dist_sq / 8.0
    envelope = envelope_base * envelope_base
    d_readout = envelope * weights
    d_pre = (d_readout[:, None] * out_weight[None, :] * silu_slope(pre)).astype(jnp.bfloat16)
    d_latent = lax.dot_general(d_pre, mix_weight, (((1,), (1,)), ((), ())), preferred_element_type=jnp.float32)
    d_summed = (d_latent * silu_slope(summed)).astype(jnp.bfloat16)
    d_basis = lax.dot_general(radial_weight, d_summed, (((1,), (1,)), ((), ())), preferred_element_type=jnp.float32)
    d_dist = jnp.sum(d_basis * basis_exact * (-4.0 * offset), axis=0)
    d_dist = d_dist + readout * weights * 2.0 * envelope_base * (-0.125)
    d_dist = d_dist.reshape(slots, slots)
    pull = 2.0 * diff * d_dist[None, :, :]
    return jnp.sum(pull, axis=2), -jnp.sum(pull, axis=1)


def live_mask(count):
    return (jnp.arange(CELL, dtype=jnp.int32) < count).astype(jnp.float32)


def reference(positions, features, tile_first, tile_second, count_first, count_second, w_first, w_second, radial_weight, mix_weight, out_weight):
    first_all = project(features, w_first)
    second_all = project(features, w_second)
    pos_all = positions.astype(jnp.float32)
    owner = (jnp.arange(TILES, dtype=jnp.int32) // TILE_DEV).astype(jnp.int32)
    group = owner // N_DEV
    member = owner % N_DEV
    block = tile_second // CELLS_DEV
    other = ((group - block // 2) % N_GRP) * N_DEV + (member - block % 2) % N_DEV
    first_cell = (owner * CELLS_DEV + tile_first).astype(jnp.int32)
    second_cell = (other * CELLS_DEV + tile_second % CELLS_DEV).astype(jnp.int32)

    def visit(total, item):
        cell_a, cell_b, num_a, num_b = item
        start_a = (cell_a * CELL).astype(jnp.int32)
        start_b = (cell_b * CELL).astype(jnp.int32)
        pos_a = lax.dynamic_slice_in_dim(pos_all, start_a, CELL, 1)
        pos_b = lax.dynamic_slice_in_dim(pos_all, start_b, CELL, 1)
        proj_a = lax.dynamic_slice_in_dim(first_all, start_a, CELL, 0)
        proj_b = lax.dynamic_slice_in_dim(second_all, start_b, CELL, 0)
        grad_a, grad_b = tile_gradients(pos_a, pos_b, proj_a, proj_b, live_mask(num_a), live_mask(num_b), radial_weight, mix_weight, out_weight)
        total = lax.dynamic_update_slice_in_dim(total, lax.dynamic_slice_in_dim(total, start_a, CELL, 1) + grad_a, start_a, 1)
        total = lax.dynamic_update_slice_in_dim(total, lax.dynamic_slice_in_dim(total, start_b, CELL, 1) + grad_b, start_b, 1)
        return total, None

    start = jnp.zeros((3, BEADS), jnp.float32)
    total, unused = lax.scan(visit, start, (first_cell, second_cell, count_first, count_second))
    return -total
```

```python
import jax
import jax.numpy as jnp
from jax import lax
from jax.experimental import pallas as pl
from jax.experimental.pallas import tpu as pltpu
from jax.sharding import PartitionSpec as P

CELL = 128
CELLS = 32
LAT = 128
NB = 16
ROWS = 16
PIECE = 2
SLAB = CELL + 16
SPREAD = 2.8853900817779268**0.5
STEP = 6.75 / NB
F32 = jnp.float32
BF = jnp.bfloat16


def dot(a, b, dims):
    return lax.dot_general(a, b, (dims, ((), ())), preferred_element_type=F32)


def cell_slots(cell):
    return pl.ds(pl.multiple_of(cell * CELL, CELL), CELL)


def pick_kernel(ask1, ask2, ask3, pos_ref, feat_ref, out1, out2, out3):
    tiles = out1.shape[0]

    def one(t, _):
        for ask, out in ((ask1, out1), (ask2, out2), (ask3, out3)):
            slots = cell_slots(lax.rem(ask[t], CELLS))
            out[t, :CELL] = feat_ref[slots, :]
            xyz = pos_ref[:, slots].astype(F32)
            out[t, CELL:] = jnp.concatenate([xyz, jnp.zeros((13, CELL), F32)], axis=0).astype(BF)
        return 0

    lax.fori_loop(0, tiles, one, 0)


def tile_kernel(
    tf_ref, ts_ref, ca_ref, cb_ref, pos_ref, feat_ref, got1, got2, got3, wa_ref, wb_ref, wr_ref, mix_ref, ow_ref,
    own_ref, gb_ref,
    fb_ref, xb_ref, mixt_ref, back_ref, owb_ref, lead, projc, d_ref, r2_ref, diff_ref, h_s, h2_s, y_s, slope_s, z_s,
):
    W = ROWS * CELL
    PW = PIECE * CELL
    tiles = gb_ref.shape[0]

    ow = ow_ref[...]
    mix = mix_ref[...].astype(F32)
    mixt_ref[...] = (mix.T * 0.5).astype(BF)
    back_ref[:LAT] = jnp.concatenate([mix, jnp.zeros((LAT, LAT), F32)], axis=1).astype(BF)
    back_ref[LAT:] = jnp.concatenate([jnp.zeros((16, LAT), F32), jnp.ones((16, LAT), F32)], axis=1).astype(BF)
    owb_ref[...] = jnp.broadcast_to(ow, (CELL, LAT)).T

    own_ref[...] = jnp.zeros_like(own_ref)

    def fetch(t, _):
        slots = cell_slots(lax.rem(ts_ref[t], CELLS))
        source = ts_ref[t] // CELLS

        @pl.when(source == 0)
        def _():
            fb_ref[t] = feat_ref[slots, :]
            xb_ref[t] = pos_ref[:, slots].astype(F32)

        for k, got in ((1, got1), (2, got2), (3, got3)):

            @pl.when(source == k)
            def _():
                fb_ref[t] = got[t, :CELL]
                xb_ref[t] = got[t, CELL:].astype(F32)[:3]

        return 0

    lax.fori_loop(0, tiles, fetch, 0)

    def prepare(t):
        swap = cb_ref[t] < ca_ref[t]
        slots = cell_slots(tf_ref[t])
        proj_a = dot(feat_ref[slots, :], wa_ref[...], ((1,), (0,))).astype(BF).astype(F32)
        proj_b = dot(fb_ref[t], wb_ref[...], ((1,), (0,))).astype(BF).astype(F32)
        pr = jnp.where(swap, proj_b, proj_a) * 0.5
        pc = jnp.where(swap, proj_a, proj_b) * 0.5
        projc[t] = pc.T
        lead[t] = pr.reshape(CELL // ROWS, ROWS, LAT).astype(BF)
        xa = pos_ref[:, slots].astype(F32)
        xb = xb_ref[t]
        xr = jnp.where(swap, xb, xa)
        xc = jnp.where(swap, xa, xb)
        r2 = jnp.zeros((CELL, CELL), F32)
        for k in range(3):
            d = jnp.broadcast_to(xr[k : k + 1], (CELL, CELL)).T - jnp.broadcast_to(xc[k : k + 1], (CELL, CELL))
            diff_ref[t, k] = d
            r2 = r2 + d * d
        r2_ref[t] = r2 * SPREAD

    def prepare_two(u, _):
        prepare(2 * u)
        prepare(2 * u + 1)
        return 0

    lax.fori_loop(0, tiles // 2, prepare_two, 0)

    hot = lax.broadcasted_iota(jnp.int32, (ROWS, W), 0) == lax.broadcasted_iota(jnp.int32, (ROWS, W), 1) // CELL
    hot = hot.astype(F32).astype(BF)
    centers = lax.broadcasted_iota(jnp.int32, (NB, CELL), 0).astype(F32) * (STEP * SPREAD)

    def steps_of(t):
        return (jnp.minimum(ca_ref[t], cb_ref[t]) + ROWS - 1) // ROWS

    def step(it, carry):
        t1, c1, t2, c2, t3, c3, t4, c4 = carry
        rows = lambda c: pl.ds(pl.multiple_of(c * ROWS, ROWS), ROWS)
        in1 = jnp.minimum(t1, tiles - 1)
        in2 = jnp.minimum(t2, tiles - 1)
        slope_at = lax.rem(it, 2)
        z_at = lax.rem(it, 3)
        r2 = r2_ref[in1, rows(c1), :]
        lhs = jnp.concatenate([wr_ref[...] * jnp.asarray(0.5, BF), lead[in1, c1]], axis=0)
        pc = jnp.concatenate([projc[in2]] * PIECE, axis=1)
        owb = jnp.concatenate([owb_ref[...]] * PIECE, axis=1)
        cores = []
        readouts = []
        for p in range(ROWS // PIECE):
            cs = slice(p * PW, (p + 1) * PW)
            ds = (y_s[:, cs] * slope_s[slope_at, :, cs]).astype(BF)
            z = dot(wr_ref[...], ds, ((1,), (0,))) * z_s[z_at, :, cs]
            cores += [jnp.sum(z[:, i * CELL : (i + 1) * CELL], axis=0, keepdims=True) for i in range(PIECE)]
            h2 = h2_s[:, cs]
            tt = jnp.tanh(h2)
            v = owb * (1 + tt)
            act = h2 * v
            y = dot(back_ref[...], jnp.concatenate([v + act * (1 - tt), act], axis=0).astype(BF), ((1,), (0,)))
            y_s[:, cs] = y[:LAT]
            ro = y[LAT : LAT + 1]
            readouts += [ro[:, i * CELL : (i + 1) * CELL] for i in range(PIECE)]
            h = h_s[:, cs] + pc
            tt = jnp.tanh(h)
            v = 1 + tt
            act = h * v
            slope_s[slope_at, :, cs] = v + act * (1 - tt)
            h2_s[:, cs] = dot(mixt_ref[...], act.astype(BF), ((1,), (0,)))
            gs = []
            zs = []
            for i in range(p * PIECE, (p + 1) * PIECE):
                o = jnp.broadcast_to(r2[i : i + 1], (NB, CELL)) - centers
                g = jnp.exp2(-(o * o))
                gs.append(g.astype(BF))
                zs.append(g * o)
            z_s[z_at, :, cs] = jnp.concatenate(zs, axis=1)
            rhs = jnp.concatenate([jnp.concatenate(gs, axis=1), hot[:, cs]], axis=0)
            h_s[:, cs] = dot(lhs, rhs, ((0,), (0,)))
        d_ref[0, t4, rows(c4), :] = jnp.concatenate(cores, axis=0)
        d_ref[1, t3, rows(c3), :] = jnp.concatenate(readouts, axis=0)
        last = c1 + 1 >= steps_of(in1)
        return (
            jnp.where(last, jnp.minimum(t1 + 1, tiles), t1), jnp.where(last, 0, c1 + 1), t1, c1, t2, c2, t3, c3,
        )

    total = jnp.int32(3)
    for t in range(tiles):
        total = total + steps_of(t)
    none = jnp.int32(tiles)
    zero = jnp.int32(0)
    lax.fori_loop(0, total, step, (zero, zero, none, zero, none, zero, none, zero))

    def finish(t):
        ca, cb = ca_ref[t], cb_ref[t]
        swap = cb < ca
        row = lax.broadcasted_iota(jnp.int32, (CELL, CELL), 0)
        col = lax.broadcasted_iota(jnp.int32, (CELL, CELL), 1)
        live = (row < jnp.minimum(ca, cb)) & (col < jnp.maximum(ca, cb))
        env = 1 - r2_ref[t] * (0.125 / SPREAD)
        dd = env * env * (d_ref[0, t] * (-4.0 / (SPREAD * 4 * CELL))) + env * (d_ref[1, t] * (-0.25 / CELL))
        dd = jnp.where(live, 2 * dd, 0.0)
        gr = []
        gc = []
        for k in range(3):
            pull = diff_ref[t, k] * dd
            gr.append(jnp.sum(pull.T, axis=0, keepdims=True))
            gc.append(-jnp.sum(pull, axis=0, keepdims=True))
        gr = jnp.concatenate(gr, axis=0)
        gc = jnp.concatenate(gc, axis=0)
        return jnp.where(swap, gc, gr), jnp.where(swap, gr, gc)

    def put(t, ga, gb):
        own_ref[:, cell_slots(tf_ref[t])] -= ga
        gb_ref[t] = gb

        @pl.when(ts_ref[t] // CELLS == 0)
        def _():
            own_ref[:, cell_slots(lax.rem(ts_ref[t], CELLS))] -= gb

    def finish_two(u, _):
        one = finish(2 * u)
        two = finish(2 * u + 1)
        put(2 * u, *one)
        put(2 * u + 1, *two)
        return 0

    lax.fori_loop(0, tiles // 2, finish_two, 0)


def sum_kernel(ask1, ask2, ask3, own_ref, back1, back2, back3, out_ref):
    out_ref[...] = own_ref[...]

    def one(t, _):
        for k, ask, back in ((1, ask1, back1), (2, ask2, back2), (3, ask3, back3)):

            @pl.when(ask[t] // CELLS == k)
            def _():
                out_ref[:, cell_slots(lax.rem(ask[t], CELLS))] -= back[t]

        return 0

    lax.fori_loop(0, back1.shape[0], one, 0)


def on_device(
    positions, features, tile_first, tile_second, count_first, count_second, w_first, w_second, radial_weight,
    mix_weight, out_weight,
):
    n_grp = lax.axis_size("grp")
    n_dev = lax.axis_size("dev")
    tiles = tile_first.shape[0]
    smem = pl.BlockSpec(memory_space=pltpu.SMEM)
    vmem = pl.BlockSpec(memory_space=pltpu.VMEM)

    def moved(array, by_grp, by_dev):
        pairs = []
        for g in range(n_grp):
            for d in range(n_dev):
                pairs.append((g * n_dev + d, (g + by_grp) % n_grp * n_dev + (d + by_dev) % n_dev))
        return lax.ppermute(array, ("grp", "dev"), pairs)

    ways = ((0, 1), (1, 0), (1, 1))
    asks = [moved(tile_second, -g, -d) for g, d in ways]
    sent = pl.pallas_call(
        pick_kernel,
        out_shape=[jax.ShapeDtypeStruct((tiles, SLAB, LAT), BF)] * 3,
        in_specs=[smem] * 3 + [vmem] * 2,
        out_specs=[vmem] * 3,
        name="pick",
    )(*asks, positions, features)
    got = [moved(array, g, d) for array, (g, d) in zip(sent, ways)]
    W = ROWS * CELL
    own, second = pl.pallas_call(
        tile_kernel,
        out_shape=[jax.ShapeDtypeStruct(positions.shape, F32), jax.ShapeDtypeStruct((tiles, 3, CELL), F32)],
        in_specs=[smem] * 4 + [vmem] * 10,
        out_specs=[vmem] * 2,
        scratch_shapes=[
            pltpu.VMEM((tiles, CELL, LAT), BF),
            pltpu.VMEM((tiles, 3, CELL), F32),
            pltpu.VMEM((LAT, LAT), BF),
            pltpu.VMEM((LAT + 16, 2 * LAT), BF),
            pltpu.VMEM((LAT, CELL), F32),
            pltpu.VMEM((tiles, CELL // ROWS, ROWS, LAT), BF),
            pltpu.VMEM((tiles, LAT, CELL), F32),
            pltpu.VMEM((2, tiles + 1, CELL, CELL), F32),
            pltpu.VMEM((tiles, CELL, CELL), F32),
            pltpu.VMEM((tiles, 3, CELL, CELL), F32),
            pltpu.VMEM((LAT, W), F32),
            pltpu.VMEM((LAT, W), F32),
            pltpu.VMEM((LAT, W), F32),
            pltpu.VMEM((2, LAT, W), F32),
            pltpu.VMEM((3, NB, W), F32),
        ],
        compiler_params=pltpu.CompilerParams(vmem_limit_bytes=40 << 20),
        name="tiles",
    )(
        tile_first, tile_second, count_first, count_second, positions, features, *got, w_first, w_second,
        radial_weight, mix_weight, out_weight.reshape(1, LAT),
    )
    returned = [moved(second, -g, -d) for g, d in ways]
    return pl.pallas_call(
        sum_kernel,
        out_shape=jax.ShapeDtypeStruct(positions.shape, F32),
        in_specs=[smem] * 3 + [vmem] * 4,
        out_specs=vmem,
        name="sum",
    )(*asks, own, *returned)


def solution(mesh):
    each = P(("grp", "dev"))
    in_specs = (P(None, ("grp", "dev")), P(("grp", "dev"), None), each, each, each, each, P(), P(), P(), P(), P())
    return jax.shard_map(
        on_device, mesh=mesh, in_specs=in_specs, out_specs=P(None, ("grp", "dev")), check_vma=False
    )
```

```python
import functools

import jax
import jax.numpy as jnp
from jax import lax
from jax.experimental import pallas as pl
from jax.experimental.pallas import tpu as pltpu
from jax.sharding import PartitionSpec as P

CELL = 128
CELLS = 32
LAT = 128
NB = 16
ROWS = 16
SUB = 8
PIECE = 2
WAYS = ((0, 1), (1, 0), (1, 1))
MESH = pl.DeviceIdType.MESH
SPREAD = 2.8853900817779268**0.5
STEP = 6.75 / NB
F32 = jnp.float32
BF = jnp.bfloat16


def dot(a, b, dims):
    return lax.dot_general(a, b, (dims, ((), ())), preferred_element_type=F32)


def cell_slots(cell):
    return pl.ds(pl.multiple_of(cell * CELL, CELL), CELL)


def other(by_grp, by_dev):
    g = lax.axis_index("grp") + by_grp
    d = lax.axis_index("dev") + by_dev
    n_grp = lax.axis_size("grp")
    n_dev = lax.axis_size("dev")
    return lax.rem(g + n_grp, n_grp), lax.rem(d + n_dev, n_dev)


def fetch_kernel(
    n_tiles, ts_ref, pos_ref, feat_ref, ask_ref, got_ref, gotpos_ref,
    mine, numbers, out_ref, ask_send, ask_recv, local_sem, feat_send, feat_recv, pos_send, pos_recv,
):
    barrier = pltpu.get_barrier_semaphore()
    for g, d in WAYS:
        pl.semaphore_signal(barrier, inc=1, device_id=other(g, d), device_id_type=MESH)
        pl.semaphore_signal(barrier, inc=1, device_id=other(-g, -d), device_id_type=MESH)
    for t in range(n_tiles):
        mine[t : t + 1, :] = jnp.full((1, CELL), ts_ref[t], jnp.int32)
    pl.semaphore_wait(barrier, 2 * len(WAYS))

    asks = []
    for w, (g, d) in enumerate(WAYS):
        copy = pltpu.make_async_remote_copy(
            src_ref=mine, dst_ref=ask_ref.at[w], send_sem=ask_send.at[w], recv_sem=ask_recv.at[w],
            device_id=other(-g, -d), device_id_type=MESH,
        )
        copy.start()
        asks.append(copy)
    sent = []
    for w, (g, d) in enumerate(WAYS):
        copy = pltpu.make_async_remote_copy(
            src_ref=pos_ref, dst_ref=gotpos_ref.at[w], send_sem=pos_send.at[w], recv_sem=pos_recv.at[w],
            device_id=other(g, d), device_id_type=MESH,
        )
        copy.start()
        sent.append(copy)
    for w in (2, 1, 0):
        asks[w].wait_recv()
        local = pltpu.make_async_copy(ask_ref.at[w], numbers.at[w], local_sem.at[w])
        local.start()
        local.wait()
        for t in range(n_tiles):
            out_ref[w, t] = feat_ref[lax.rem(numbers[w, t, 0], CELLS)]
        copy = pltpu.make_async_remote_copy(
            src_ref=out_ref.at[w], dst_ref=got_ref.at[w], send_sem=feat_send.at[w], recv_sem=feat_recv.at[w],
            device_id=other(*WAYS[w]), device_id_type=MESH,
        )
        copy.start()
        sent.append(copy)
    for copy in asks:
        copy.wait_send()
    for copy in sent:
        copy.wait()


def tile_kernel(
    tf_ref, ts_ref, ca_ref, cb_ref, pos_ref, feat_ref, got_ref, gotpos_ref, wa_ref, wb_ref, wr_ref, mix_ref, ow_ref,
    own_ref, gb_ref,
    fa_ref, fb_ref, xb_ref, mixt_ref, owb_ref, lead, projc, d_ref, r2_ref, diff_ref, h_s, h2_s, y_s, slope_s, z_s,
    sem_a, sem_b,
):
    W = ROWS * CELL
    PW = PIECE * CELL
    tiles = gb_ref.shape[0]

    for t in range(tiles):
        pltpu.make_async_copy(feat_ref.at[cell_slots(tf_ref[t])], fa_ref.at[t], sem_a.at[t]).start()
        slots = cell_slots(lax.rem(ts_ref[t], CELLS))
        source = ts_ref[t] // CELLS

        @pl.when(source == 0)
        def _():
            pltpu.make_async_copy(feat_ref.at[slots], fb_ref.at[t], sem_b.at[t]).start()
            xb_ref[t] = pos_ref[:, slots].astype(F32)

        @pl.when(source > 0)
        def _():
            pltpu.make_async_copy(got_ref.at[source - 1, t], fb_ref.at[t], sem_b.at[t]).start()
            xb_ref[t] = gotpos_ref[source - 1, :, slots].astype(F32)

    mixt_ref[...] = (mix_ref[...].astype(F32).T * 0.5).astype(BF)
    owb_ref[...] = jnp.broadcast_to(ow_ref[...], (CELL, LAT)).T
    own_ref[...] = jnp.zeros_like(own_ref)
    for t in range(tiles):
        pltpu.make_async_copy(feat_ref.at[pl.ds(0, CELL)], fa_ref.at[t], sem_a.at[t]).wait()
        pltpu.make_async_copy(feat_ref.at[pl.ds(0, CELL)], fb_ref.at[t], sem_b.at[t]).wait()

    def prepare(t):
        swap = cb_ref[t] < ca_ref[t]
        slots = cell_slots(tf_ref[t])
        proj_a = dot(fa_ref[t], wa_ref[...], ((1,), (0,))).astype(BF).astype(F32)
        proj_b = dot(fb_ref[t], wb_ref[...], ((1,), (0,))).astype(BF).astype(F32)
        pr = jnp.where(swap, proj_b, proj_a) * 0.5
        pc = jnp.where(swap, proj_a, proj_b) * 0.5
        projc[t] = pc.T
        groups = pr.reshape(CELL // SUB, SUB, LAT)
        lead[t] = jnp.concatenate([groups, jnp.zeros_like(groups)], axis=1).astype(BF)
        xa = pos_ref[:, slots].astype(F32)
        xb = xb_ref[t]
        xr = jnp.where(swap, xb, xa)
        xc = jnp.where(swap, xa, xb)
        r2 = jnp.zeros((CELL, CELL), F32)
        for k in range(3):
            d = jnp.broadcast_to(xr[k : k + 1], (CELL, CELL)).T - jnp.broadcast_to(xc[k : k + 1], (CELL, CELL))
            diff_ref[t, k] = d
            r2 = r2 + d * d
        r2_ref[t] = r2 * SPREAD

    def prepare_two(u, _):
        prepare(2 * u)
        prepare(2 * u + 1)
        return 0

    lax.fori_loop(0, tiles // 2, prepare_two, 0)

    hot = lax.broadcasted_iota(jnp.int32, (16, SUB * CELL), 0)
    hot = hot == lax.broadcasted_iota(jnp.int32, (16, SUB * CELL), 1) // CELL
    hot = hot.astype(F32).astype(BF)
    centers = lax.broadcasted_iota(jnp.int32, (NB, CELL), 0).astype(F32) * (STEP * SPREAD)
    n_sub = ROWS // SUB
    per_sub = SUB // PIECE

    def subs_of(t):
        return (jnp.minimum(ca_ref[t], cb_ref[t]) + SUB - 1) // SUB

    def following(place):
        places = []
        for _ in range(n_sub):
            t, c = place
            last = c + 1 >= subs_of(jnp.minimum(t, tiles - 1))
            place = jnp.where(last, jnp.minimum(t + 1, tiles), t), jnp.where(last, 0, c + 1)
            places.append(place)
        return tuple(places)

    def step(it, carry):
        at1, at2, at3, at4 = carry
        rows = lambda c: pl.ds(pl.multiple_of(c * SUB, SUB), SUB)
        slope_at = lax.rem(it, 2)
        z_at = lax.rem(it, 3)
        owb = jnp.concatenate([owb_ref[...]] * PIECE, axis=1)
        for p in range(ROWS // PIECE):
            cs = slice(p * PW, (p + 1) * PW)
            q = p % per_sub
            if q == 0:
                (t1, c1), (t2, _), (t3, c3), (t4, c4) = (at[p // per_sub] for at in carry)
                in1 = jnp.minimum(t1, tiles - 1)
                r2 = r2_ref[in1, rows(c1), :]
                lhs = jnp.concatenate([wr_ref[...] * jnp.asarray(0.5, BF), lead[in1, c1]], axis=0)
                pc = jnp.concatenate([projc[jnp.minimum(t2, tiles - 1)]] * PIECE, axis=1)
                cores = []
                readouts = []
            ds = (y_s[:, cs] * slope_s[slope_at, :, cs]).astype(BF)
            z = dot(wr_ref[...], ds, ((1,), (0,))) * z_s[z_at, :, cs]
            cores += [jnp.sum(z[:, i * CELL : (i + 1) * CELL], axis=0, keepdims=True) for i in range(PIECE)]
            h2 = h2_s[:, cs]
            tt = jnp.tanh(h2)
            v = owb * (1 + tt)
            act = h2 * v
            y_s[:, cs] = dot(mix_ref[...], (v + act * (1 - tt)).astype(BF), ((1,), (0,)))
            ro = jnp.sum(act, axis=0, keepdims=True)
            readouts += [ro[:, i * CELL : (i + 1) * CELL] for i in range(PIECE)]
            h = h_s[:, cs] + pc
            tt = jnp.tanh(h)
            v = 1 + tt
            act = h * v
            slope_s[slope_at, :, cs] = v + act * (1 - tt)
            h2_s[:, cs] = dot(mixt_ref[...], act.astype(BF), ((1,), (0,)))
            gs = []
            zs = []
            for i in range(q * PIECE, (q + 1) * PIECE):
                o = jnp.broadcast_to(r2[i : i + 1], (NB, CELL)) - centers
                g = jnp.exp2(-(o * o))
                gs.append(g.astype(BF))
                zs.append(g * o)
            z_s[z_at, :, cs] = jnp.concatenate(zs, axis=1)
            rhs = jnp.concatenate([jnp.concatenate(gs, axis=1), hot[:, q * PW : (q + 1) * PW]], axis=0)
            h_s[:, cs] = dot(lhs, rhs, ((0,), (0,)))
            if q == per_sub - 1:
                d_ref[0, t4, rows(c4), :] = jnp.concatenate(cores, axis=0)
                d_ref[1, t3, rows(c3), :] = jnp.concatenate(readouts, axis=0)
        return following(at1[-1]), at1, at2, at3

    total = jnp.int32(0)
    for t in range(tiles):
        total = total + subs_of(t)
    zero = jnp.int32(0)
    start = (zero, zero)
    start = ((start,) + following(start))[:n_sub]
    idle = ((jnp.int32(tiles), zero),) * n_sub
    lax.fori_loop(0, (total + n_sub - 1) // n_sub + 3, step, (start, idle, idle, idle))

    def finish(t):
        ca, cb = ca_ref[t], cb_ref[t]
        swap = cb < ca
        row = lax.broadcasted_iota(jnp.int32, (CELL, CELL), 0)
        col = lax.broadcasted_iota(jnp.int32, (CELL, CELL), 1)
        live = (row < jnp.minimum(ca, cb)) & (col < jnp.maximum(ca, cb))
        env = 1 - r2_ref[t] * (0.125 / SPREAD)
        dd = env * env * (d_ref[0, t] * (-4.0 / (SPREAD * 4 * CELL))) + env * (d_ref[1, t] * (-0.25 / CELL))
        dd = jnp.where(live, 2 * dd, 0.0)
        gr = []
        gc = []
        for k in range(3):
            pull = diff_ref[t, k] * dd
            gr.append(jnp.sum(pull.T, axis=0, keepdims=True))
            gc.append(-jnp.sum(pull, axis=0, keepdims=True))
        gr = jnp.concatenate(gr, axis=0)
        gc = jnp.concatenate(gc, axis=0)
        return jnp.where(swap, gc, gr), jnp.where(swap, gr, gc)

    def put(t, ga, gb):
        own_ref[:, cell_slots(tf_ref[t])] -= ga
        gb_ref[t] = gb

        @pl.when(ts_ref[t] // CELLS == 0)
        def _():
            own_ref[:, cell_slots(lax.rem(ts_ref[t], CELLS))] -= gb

    def finish_two(u, _):
        one = finish(2 * u)
        two = finish(2 * u + 1)
        put(2 * u, *one)
        put(2 * u + 1, *two)
        return 0

    lax.fori_loop(0, tiles // 2, finish_two, 0)


def return_kernel(n_tiles, ask_ref, own_ref, second_ref, out_ref, back_ref, send_sem, recv_sem):
    barrier = pltpu.get_barrier_semaphore()
    for g, d in WAYS:
        pl.semaphore_signal(barrier, inc=1, device_id=other(g, d), device_id_type=MESH)
    pl.semaphore_wait(barrier, len(WAYS))
    copies = []
    for w, (g, d) in enumerate(WAYS):
        copy = pltpu.make_async_remote_copy(
            src_ref=second_ref, dst_ref=back_ref.at[w], send_sem=send_sem.at[w], recv_sem=recv_sem.at[w],
            device_id=other(-g, -d), device_id_type=MESH,
        )
        copy.start()
        copies.append(copy)
    for copy in copies:
        copy.wait()

    def one(c, _):
        slots = cell_slots(c)
        total = own_ref[:, slots]
        for w in range(len(WAYS)):
            for t in range(n_tiles):
                total -= jnp.where(ask_ref[w, t : t + 1, :] == (w + 1) * CELLS + c, back_ref[w, t], 0.0)
        out_ref[:, slots] = total
        return 0

    lax.fori_loop(0, CELLS, one, 0)


def on_device(
    positions, features, tile_first, tile_second, count_first, count_second, w_first, w_second, radial_weight,
    mix_weight, out_weight,
):
    tiles = tile_first.shape[0]
    smem = pl.BlockSpec(memory_space=pltpu.SMEM)
    vmem = pl.BlockSpec(memory_space=pltpu.VMEM)

    anywhere = pl.BlockSpec(memory_space=pl.ANY)
    dma = pltpu.SemaphoreType.DMA
    n = len(WAYS)
    ask, got, got_pos = pl.pallas_call(
        functools.partial(fetch_kernel, tiles),
        out_shape=[
            jax.ShapeDtypeStruct((n, tiles, CELL), jnp.int32),
            jax.ShapeDtypeStruct((n, tiles, CELL, LAT), BF),
            jax.ShapeDtypeStruct((n, *positions.shape), BF),
        ],
        in_specs=[smem, vmem, vmem],
        out_specs=[vmem, anywhere, vmem],
        scratch_shapes=[
            pltpu.VMEM((tiles, CELL), jnp.int32),
            pltpu.SMEM((n, tiles, CELL), jnp.int32),
            pltpu.VMEM((n, tiles, CELL, LAT), BF),
        ]
        + [dma((n,))] * 7,
        compiler_params=pltpu.CompilerParams(collective_id=0, has_side_effects=True),
        name="fetch",
    )(tile_second, positions, features.reshape(-1, CELL, LAT))
    W = ROWS * CELL
    own, second = pl.pallas_call(
        tile_kernel,
        out_shape=[jax.ShapeDtypeStruct(positions.shape, F32), jax.ShapeDtypeStruct((tiles, 3, CELL), F32)],
        in_specs=[smem] * 4 + [vmem, anywhere, anywhere] + [vmem] * 6,
        out_specs=[vmem] * 2,
        scratch_shapes=[
            pltpu.VMEM((tiles, CELL, LAT), BF),
            pltpu.VMEM((tiles, CELL, LAT), BF),
            pltpu.VMEM((tiles, 3, CELL), F32),
            pltpu.VMEM((LAT, LAT), BF),
            pltpu.VMEM((LAT, CELL), F32),
            pltpu.VMEM((tiles, CELL // SUB, 16, LAT), BF),
            pltpu.VMEM((tiles, LAT, CELL), F32),
            pltpu.VMEM((2, tiles + 1, CELL, CELL), F32),
            pltpu.VMEM((tiles, CELL, CELL), F32),
            pltpu.VMEM((tiles, 3, CELL, CELL), F32),
            pltpu.VMEM((LAT, W), F32),
            pltpu.VMEM((LAT, W), F32),
            pltpu.VMEM((LAT, W), F32),
            pltpu.VMEM((2, LAT, W), F32),
            pltpu.VMEM((3, NB, W), F32),
            dma((tiles,)),
            dma((tiles,)),
        ],
        compiler_params=pltpu.CompilerParams(vmem_limit_bytes=40 << 20),
        name="tiles",
    )(
        tile_first, tile_second, count_first, count_second, positions, features, got, got_pos, w_first, w_second,
        radial_weight, mix_weight, out_weight.reshape(1, LAT),
    )
    return pl.pallas_call(
        functools.partial(return_kernel, tiles),
        out_shape=jax.ShapeDtypeStruct(positions.shape, F32),
        in_specs=[vmem] * 3,
        out_specs=vmem,
        scratch_shapes=[pltpu.VMEM((n, tiles, 3, CELL), F32), dma((n,)), dma((n,))],
        compiler_params=pltpu.CompilerParams(collective_id=1, has_side_effects=True),
        name="return",
    )(ask, own, second)


def solution(mesh):
    each = P(("grp", "dev"))
    in_specs = (P(None, ("grp", "dev")), P(("grp", "dev"), None), each, each, each, each, P(), P(), P(), P(), P())
    return jax.shard_map(
        on_device, mesh=mesh, in_specs=in_specs, out_specs=P(None, ("grp", "dev")), check_vma=False
    )
```

```python
import functools

import jax
import jax.numpy as jnp
from jax import lax
from jax.experimental import pallas as pl
from jax.experimental.pallas import tpu as pltpu
from jax.sharding import PartitionSpec as P

CELL = 128
CELLS = 32
LAT = 128
NB = 16
ROWS = 16
SUB = 8
PIECE = 2
WAYS = ((0, 1), (1, 0), (1, 1))
MESH = pl.DeviceIdType.MESH
SPREAD = 2.8853900817779268**0.5
STEP = 6.75 / NB
F32 = jnp.float32
BF = jnp.bfloat16


def dot(a, b, dims):
    return lax.dot_general(a, b, (dims, ((), ())), preferred_element_type=F32)


def cell_slots(cell):
    return pl.ds(pl.multiple_of(cell * CELL, CELL), CELL)


def other(by_grp, by_dev):
    g = lax.axis_index("grp") + by_grp
    d = lax.axis_index("dev") + by_dev
    n_grp = lax.axis_size("grp")
    n_dev = lax.axis_size("dev")
    return lax.rem(g + n_grp, n_grp), lax.rem(d + n_dev, n_dev)


def fetch_kernel(
    n_tiles, ts_ref, pos_ref, feat_any, ask_ref, got_ref, gotpos_ref,
    feat_ref, feat_sem, mine, numbers, out_ref, ask_send, ask_recv, local_sem, feat_send, feat_recv, pos_send, pos_recv,
):
    features = pltpu.make_async_copy(feat_any, feat_ref, feat_sem)
    features.start()
    barrier = pltpu.get_barrier_semaphore()
    for g, d in WAYS:
        pl.semaphore_signal(barrier, inc=1, device_id=other(g, d), device_id_type=MESH)
        pl.semaphore_signal(barrier, inc=1, device_id=other(-g, -d), device_id_type=MESH)
    for t in range(n_tiles):
        mine[t : t + 1, :] = jnp.full((1, CELL), ts_ref[t], jnp.int32)
    pl.semaphore_wait(barrier, 2 * len(WAYS))

    asks = []
    for w, (g, d) in enumerate(WAYS):
        copy = pltpu.make_async_remote_copy(
            src_ref=mine, dst_ref=ask_ref.at[w], send_sem=ask_send.at[w], recv_sem=ask_recv.at[w],
            device_id=other(-g, -d), device_id_type=MESH,
        )
        copy.start()
        asks.append(copy)
    sent = []
    for w, (g, d) in enumerate(WAYS):
        copy = pltpu.make_async_remote_copy(
            src_ref=pos_ref, dst_ref=gotpos_ref.at[w], send_sem=pos_send.at[w], recv_sem=pos_recv.at[w],
            device_id=other(g, d), device_id_type=MESH,
        )
        copy.start()
        sent.append(copy)
    features.wait()
    for w in (2, 1, 0):
        asks[w].wait_recv()
        local = pltpu.make_async_copy(ask_ref.at[w], numbers.at[w], local_sem.at[w])
        local.start()
        local.wait()
        for t in range(n_tiles):
            out_ref[w, t] = feat_ref[lax.rem(numbers[w, t, 0], CELLS)]
        copy = pltpu.make_async_remote_copy(
            src_ref=out_ref.at[w], dst_ref=got_ref.at[w], send_sem=feat_send.at[w], recv_sem=feat_recv.at[w],
            device_id=other(*WAYS[w]), device_id_type=MESH,
        )
        copy.start()
        sent.append(copy)
    for copy in asks:
        copy.wait_send()
    for copy in sent:
        copy.wait()


def tile_kernel(
    tf_ref, ts_ref, ca_ref, cb_ref, pos_any, feat_ref, got_ref, gotpos_any, wa_any, wb_any, wr_any, mix_any, ow_any,
    own_ref, gb_ref,
    pos_ref, gotpos_ref, wa_ref, wb_ref, wr_ref, mix_ref, ow_ref,
    fa_ref, fb_ref, xb_ref, mixt_ref, owb_ref, lead, projc, d_ref, r2_ref, diff_ref, h_s, h2_s, y_s, slope_s, z_s,
    sem_a, sem_b, sem_c,
):
    W = ROWS * CELL
    PW = PIECE * CELL
    tiles = gb_ref.shape[0]

    loads = []
    for src, dst in (
        (pos_any, pos_ref), (gotpos_any, gotpos_ref), (wa_any, wa_ref), (wb_any, wb_ref), (wr_any, wr_ref),
        (mix_any, mix_ref), (ow_any, ow_ref),
    ):
        loads.append(pltpu.make_async_copy(src, dst, sem_c.at[len(loads)]))
        loads[-1].start()
    for t in range(tiles):
        pltpu.make_async_copy(feat_ref.at[cell_slots(tf_ref[t])], fa_ref.at[t], sem_a.at[t]).start()
        slots = cell_slots(lax.rem(ts_ref[t], CELLS))
        source = ts_ref[t] // CELLS

        @pl.when(source == 0)
        def _():
            pltpu.make_async_copy(feat_ref.at[slots], fb_ref.at[t], sem_b.at[t]).start()

        @pl.when(source > 0)
        def _():
            pltpu.make_async_copy(got_ref.at[source - 1, t], fb_ref.at[t], sem_b.at[t]).start()

    for load in loads:
        load.wait()
    for t in range(tiles):
        slots = cell_slots(lax.rem(ts_ref[t], CELLS))
        source = ts_ref[t] // CELLS
        came = gotpos_ref[jnp.maximum(source - 1, 0), :, slots].astype(F32)
        xb_ref[t] = jnp.where(source == 0, pos_ref[:, slots].astype(F32), came)
    mixt_ref[...] = (mix_ref[...].astype(F32).T * 0.5).astype(BF)
    owb_ref[...] = jnp.broadcast_to(ow_ref[...], (CELL, LAT)).T
    own_ref[...] = jnp.zeros_like(own_ref)
    for t in range(tiles):
        pltpu.make_async_copy(feat_ref.at[pl.ds(0, CELL)], fa_ref.at[t], sem_a.at[t]).wait()
        pltpu.make_async_copy(feat_ref.at[pl.ds(0, CELL)], fb_ref.at[t], sem_b.at[t]).wait()

    def prepare(t):
        swap = cb_ref[t] < ca_ref[t]
        slots = cell_slots(tf_ref[t])
        proj_a = dot(fa_ref[t], wa_ref[...], ((1,), (0,))).astype(BF).astype(F32)
        proj_b = dot(fb_ref[t], wb_ref[...], ((1,), (0,))).astype(BF).astype(F32)
        pr = jnp.where(swap, proj_b, proj_a) * 0.5
        pc = jnp.where(swap, proj_a, proj_b) * 0.5
        projc[t] = pc.T
        groups = pr.reshape(CELL // SUB, SUB, LAT)
        lead[t] = jnp.concatenate([groups, jnp.zeros_like(groups)], axis=1).astype(BF)
        xa = pos_ref[:, slots].astype(F32)
        xb = xb_ref[t]
        xr = jnp.where(swap, xb, xa)
        xc = jnp.where(swap, xa, xb)
        r2 = jnp.zeros((CELL, CELL), F32)
        for k in range(3):
            d = jnp.broadcast_to(xr[k : k + 1], (CELL, CELL)).T - jnp.broadcast_to(xc[k : k + 1], (CELL, CELL))
            diff_ref[t, k] = d
            r2 = r2 + d * d
        r2_ref[t] = r2 * SPREAD

    def prepare_two(u, _):
        prepare(2 * u)
        prepare(2 * u + 1)
        return 0

    lax.fori_loop(0, tiles // 2, prepare_two, 0)

    hot = lax.broadcasted_iota(jnp.int32, (16, SUB * CELL), 0)
    hot = hot == lax.broadcasted_iota(jnp.int32, (16, SUB * CELL), 1) // CELL
    hot = hot.astype(F32).astype(BF)
    centers = lax.broadcasted_iota(jnp.int32, (NB, CELL), 0).astype(F32) * (STEP * SPREAD)
    n_sub = ROWS // SUB
    per_sub = SUB // PIECE

    def subs_of(t):
        return (jnp.minimum(ca_ref[t], cb_ref[t]) + SUB - 1) // SUB

    def following(place):
        places = []
        for _ in range(n_sub):
            t, c = place
            last = c + 1 >= subs_of(jnp.minimum(t, tiles - 1))
            place = jnp.where(last, jnp.minimum(t + 1, tiles), t), jnp.where(last, 0, c + 1)
            places.append(place)
        return tuple(places)

    def step(it, carry):
        at1, at2, at3, at4 = carry
        rows = lambda c: pl.ds(pl.multiple_of(c * SUB, SUB), SUB)
        slope_at = lax.rem(it, 2)
        z_at = lax.rem(it, 3)
        owb = jnp.concatenate([owb_ref[...]] * PIECE, axis=1)
        for p in range(ROWS // PIECE):
            cs = slice(p * PW, (p + 1) * PW)
            q = p % per_sub
            if q == 0:
                (t1, c1), (t2, _), (t3, c3), (t4, c4) = (at[p // per_sub] for at in carry)
                in1 = jnp.minimum(t1, tiles - 1)
                r2 = r2_ref[in1, rows(c1), :]
                lhs = jnp.concatenate([wr_ref[...] * jnp.asarray(0.5, BF), lead[in1, c1]], axis=0)
                pc = jnp.concatenate([projc[jnp.minimum(t2, tiles - 1)]] * PIECE, axis=1)
                cores = []
                readouts = []
            ds = (y_s[:, cs] * slope_s[slope_at, :, cs]).astype(BF)
            z = z_s[z_at, :, cs]
            h2 = h2_s[:, cs]
            tt = jnp.tanh(h2)
            v = owb * (1 + tt)
            act = h2 * v
            ro = jnp.sum(act, axis=0, keepdims=True)
            back = (v + act * (1 - tt)).astype(BF)
            h = h_s[:, cs] + pc
            tt = jnp.tanh(h)
            v = 1 + tt
            act = h * v
            slope_s[slope_at, :, cs] = v + act * (1 - tt)
            latent = act.astype(BF)
            gs = []
            zs = []
            for i in range(q * PIECE, (q + 1) * PIECE):
                o = jnp.broadcast_to(r2[i : i + 1], (NB, CELL)) - centers
                g = jnp.exp2(-(o * o))
                gs.append(g.astype(BF))
                zs.append(g * o)
            z_s[z_at, :, cs] = jnp.concatenate(zs, axis=1)
            rhs = jnp.concatenate([jnp.concatenate(gs, axis=1), hot[:, q * PW : (q + 1) * PW]], axis=0)
            y_s[:, cs] = dot(mix_ref[...], back, ((1,), (0,)))
            h_s[:, cs] = dot(lhs, rhs, ((0,), (0,)))
            z = dot(wr_ref[...], ds, ((1,), (0,))) * z
            h2_s[:, cs] = dot(mixt_ref[...], latent, ((1,), (0,)))
            for i in range(PIECE):
                cores.append(jnp.sum(z[:, i * CELL : (i + 1) * CELL], axis=0, keepdims=True))
                readouts.append(ro[:, i * CELL : (i + 1) * CELL])
            if q == per_sub - 1:
                d_ref[0, t4, rows(c4), :] = jnp.concatenate(cores, axis=0)
                d_ref[1, t3, rows(c3), :] = jnp.concatenate(readouts, axis=0)
        return following(at1[-1]), at1, at2, at3

    total = jnp.int32(0)
    for t in range(tiles):
        total = total + subs_of(t)
    zero = jnp.int32(0)
    start = (zero, zero)
    start = ((start,) + following(start))[:n_sub]
    idle = ((jnp.int32(tiles), zero),) * n_sub
    lax.fori_loop(0, (total + n_sub - 1) // n_sub + 3, step, (start, idle, idle, idle))

    def finish(t):
        ca, cb = ca_ref[t], cb_ref[t]
        swap = cb < ca
        row = lax.broadcasted_iota(jnp.int32, (CELL, CELL), 0)
        col = lax.broadcasted_iota(jnp.int32, (CELL, CELL), 1)
        live = (row < jnp.minimum(ca, cb)) & (col < jnp.maximum(ca, cb))
        env = 1 - r2_ref[t] * (0.125 / SPREAD)
        dd = env * env * (d_ref[0, t] * (-4.0 / (SPREAD * 4 * CELL))) + env * (d_ref[1, t] * (-0.25 / CELL))
        dd = jnp.where(live, 2 * dd, 0.0)
        gr = []
        gc = []
        for k in range(3):
            pull = diff_ref[t, k] * dd
            gr.append(jnp.sum(pull.T, axis=0, keepdims=True))
            gc.append(-jnp.sum(pull, axis=0, keepdims=True))
        gr = jnp.concatenate(gr, axis=0)
        gc = jnp.concatenate(gc, axis=0)
        return jnp.where(swap, gc, gr), jnp.where(swap, gr, gc)

    def put(t, ga, gb):
        own_ref[:, cell_slots(tf_ref[t])] -= ga
        gb_ref[t] = gb

        @pl.when(ts_ref[t] // CELLS == 0)
        def _():
            own_ref[:, cell_slots(lax.rem(ts_ref[t], CELLS))] -= gb

    def finish_two(u, _):
        one = finish(2 * u)
        two = finish(2 * u + 1)
        put(2 * u, *one)
        put(2 * u + 1, *two)
        return 0

    lax.fori_loop(0, tiles // 2, finish_two, 0)


def return_kernel(n_tiles, ask_ref, own_ref, second_ref, out_ref, back_ref, send_sem, recv_sem):
    barrier = pltpu.get_barrier_semaphore()
    for g, d in WAYS:
        pl.semaphore_signal(barrier, inc=1, device_id=other(g, d), device_id_type=MESH)
    pl.semaphore_wait(barrier, len(WAYS))
    copies = []
    for w, (g, d) in enumerate(WAYS):
        copy = pltpu.make_async_remote_copy(
            src_ref=second_ref, dst_ref=back_ref.at[w], send_sem=send_sem.at[w], recv_sem=recv_sem.at[w],
            device_id=other(-g, -d), device_id_type=MESH,
        )
        copy.start()
        copies.append(copy)
    for copy in copies:
        copy.wait()

    def one(c, _):
        slots = cell_slots(c)
        total = own_ref[:, slots]
        for w in range(len(WAYS)):
            for t in range(n_tiles):
                total -= jnp.where(ask_ref[w, t : t + 1, :] == (w + 1) * CELLS + c, back_ref[w, t], 0.0)
        out_ref[:, slots] = total
        return 0

    lax.fori_loop(0, CELLS, one, 0)


def on_device(
    positions, features, tile_first, tile_second, count_first, count_second, w_first, w_second, radial_weight,
    mix_weight, out_weight,
):
    tiles = tile_first.shape[0]
    smem = pl.BlockSpec(memory_space=pltpu.SMEM)
    vmem = pl.BlockSpec(memory_space=pltpu.VMEM)

    anywhere = pl.BlockSpec(memory_space=pl.ANY)
    dma = pltpu.SemaphoreType.DMA
    n = len(WAYS)
    ask, got, got_pos = pl.pallas_call(
        functools.partial(fetch_kernel, tiles),
        out_shape=[
            jax.ShapeDtypeStruct((n, tiles, CELL), jnp.int32),
            jax.ShapeDtypeStruct((n, tiles, CELL, LAT), BF),
            jax.ShapeDtypeStruct((n, *positions.shape), BF),
        ],
        in_specs=[smem, anywhere, anywhere],
        out_specs=[vmem, anywhere, anywhere],
        scratch_shapes=[
            pltpu.VMEM((CELLS, CELL, LAT), BF),
            dma(()),
            pltpu.VMEM((tiles, CELL), jnp.int32),
            pltpu.SMEM((n, tiles, CELL), jnp.int32),
            pltpu.VMEM((n, tiles, CELL, LAT), BF),
        ]
        + [dma((n,))] * 7,
        compiler_params=pltpu.CompilerParams(collective_id=0, has_side_effects=True),
        name="fetch",
    )(tile_second, positions, features.reshape(-1, CELL, LAT))
    W = ROWS * CELL
    own, second = pl.pallas_call(
        tile_kernel,
        out_shape=[jax.ShapeDtypeStruct(positions.shape, F32), jax.ShapeDtypeStruct((tiles, 3, CELL), F32)],
        in_specs=[smem] * 4 + [anywhere] * 9,
        out_specs=[vmem] * 2,
        scratch_shapes=[
            pltpu.VMEM(positions.shape, BF),
            pltpu.VMEM((n, *positions.shape), BF),
            pltpu.VMEM(w_first.shape, BF),
            pltpu.VMEM(w_second.shape, BF),
            pltpu.VMEM(radial_weight.shape, BF),
            pltpu.VMEM(mix_weight.shape, BF),
            pltpu.VMEM((1, LAT), F32),
            pltpu.VMEM((tiles, CELL, LAT), BF),
            pltpu.VMEM((tiles, CELL, LAT), BF),
            pltpu.VMEM((tiles, 3, CELL), F32),
            pltpu.VMEM((LAT, LAT), BF),
            pltpu.VMEM((LAT, CELL), F32),
            pltpu.VMEM((tiles, CELL // SUB, 16, LAT), BF),
            pltpu.VMEM((tiles, LAT, CELL), F32),
            pltpu.VMEM((2, tiles + 1, CELL, CELL), F32),
            pltpu.VMEM((tiles, CELL, CELL), F32),
            pltpu.VMEM((tiles, 3, CELL, CELL), F32),
            pltpu.VMEM((LAT, W), F32),
            pltpu.VMEM((LAT, W), F32),
            pltpu.VMEM((LAT, W), F32),
            pltpu.VMEM((2, LAT, W), F32),
            pltpu.VMEM((3, NB, W), F32),
            dma((tiles,)),
            dma((tiles,)),
            dma((7,)),
        ],
        compiler_params=pltpu.CompilerParams(vmem_limit_bytes=60 << 20),
        name="tiles",
    )(
        tile_first, tile_second, count_first, count_second, positions, features, got, got_pos, w_first, w_second,
        radial_weight, mix_weight, out_weight.reshape(1, LAT),
    )
    return pl.pallas_call(
        functools.partial(return_kernel, tiles),
        out_shape=jax.ShapeDtypeStruct(positions.shape, F32),
        in_specs=[vmem] * 3,
        out_specs=vmem,
        scratch_shapes=[pltpu.VMEM((n, tiles, 3, CELL), F32), dma((n,)), dma((n,))],
        compiler_params=pltpu.CompilerParams(collective_id=1, has_side_effects=True),
        name="return",
    )(ask, own, second)


def solution(mesh):
    each = P(("grp", "dev"))
    in_specs = (P(None, ("grp", "dev")), P(("grp", "dev"), None), each, each, each, each, P(), P(), P(), P(), P())
    return jax.shard_map(
        on_device, mesh=mesh, in_specs=in_specs, out_specs=P(None, ("grp", "dev")), check_vma=False
    )
```

```python
import functools

import jax
import jax.numpy as jnp
from jax import lax
from jax.experimental import pallas as pl
from jax.experimental.pallas import tpu as pltpu
from jax.sharding import PartitionSpec as P

CELL = 128
CELLS = 32
LAT = 128
NB = 16
ROWS = 16
SUB = 8
PIECE = 2
GROUPS = 4
WAYS = ((0, 1), (1, 0), (1, 1))
MESH = pl.DeviceIdType.MESH
SPREAD = 2.8853900817779268**0.5
STEP = 6.75 / NB
F32 = jnp.float32
BF = jnp.bfloat16


def dot(a, b, dims):
    return lax.dot_general(a, b, (dims, ((), ())), preferred_element_type=F32)


def cell_slots(cell):
    return pl.ds(pl.multiple_of(cell * CELL, CELL), CELL)


def other(by_grp, by_dev):
    g = lax.axis_index("grp") + by_grp
    d = lax.axis_index("dev") + by_dev
    n_grp = lax.axis_size("grp")
    n_dev = lax.axis_size("dev")
    return lax.rem(g + n_grp, n_grp), lax.rem(d + n_dev, n_dev)


def remote(src, dst, send, recv, to):
    copy = pltpu.make_async_remote_copy(
        src_ref=src, dst_ref=dst, send_sem=send, recv_sem=recv, device_id=to, device_id_type=MESH
    )
    copy.start()
    return copy


def fetch_kernel(
    n_tiles, tf_ref, ts_ref, pos_any, feat_any, ask_ref, fa_ref, fb_ref, gotpos_ref,
    feat_ref, feat_sem, mine, numbers, corner_out, corner_in, side_out, side_in, up_out, up_in,
    ask_send, ask_recv, local_sem, corner_send, corner_recv, up_send, up_recv, side_send, side_recv, pos_send, pos_recv,
):
    features = pltpu.make_async_copy(feat_any, feat_ref, feat_sem)
    features.start()
    barrier = pltpu.get_barrier_semaphore()
    for g, d in WAYS:
        pl.semaphore_signal(barrier, inc=1, device_id=other(g, d), device_id_type=MESH)
        pl.semaphore_signal(barrier, inc=1, device_id=other(-g, -d), device_id_type=MESH)
    for t in range(n_tiles):
        mine[t : t + 1, :] = jnp.full((1, CELL), ts_ref[t], jnp.int32)
    pl.semaphore_wait(barrier, 2 * len(WAYS))

    asks = [
        remote(mine, ask_ref.at[w], ask_send.at[w], ask_recv.at[w], other(-g, -d)) for w, (g, d) in enumerate(WAYS)
    ]
    sent = [
        remote(pos_any, gotpos_ref.at[w], pos_send.at[w], pos_recv.at[w], other(g, d)) for w, (g, d) in enumerate(WAYS)
    ]
    features.wait()

    def hear(w):
        asks[w].wait_recv()
        local = pltpu.make_async_copy(ask_ref.at[w], numbers.at[w], local_sem.at[w])
        local.start()
        local.wait()

    def pick(w, t):
        return feat_ref[lax.rem(numbers[w, t, 0], CELLS)]

    hear(2)
    corners = []
    for j in range(GROUPS):
        part = range(j * n_tiles // GROUPS, (j + 1) * n_tiles // GROUPS)
        for t in part:
            corner_out[t] = pick(2, t)
        at = pl.ds(part.start, len(part))
        corners.append(
            remote(corner_out.at[at], corner_in.at[at], corner_send.at[j], corner_recv.at[j], other(0, 1))
        )
    hear(0)
    for t in range(n_tiles):
        side_out[t] = pick(0, t)
    sides = remote(side_out, side_in, side_send, side_recv, other(0, 1))
    hear(1)
    for t in range(n_tiles):
        up_out[t] = pick(1, t)
    ups = []
    for j in range(GROUPS):
        part = range(j * n_tiles // GROUPS, (j + 1) * n_tiles // GROUPS)
        corners[j].wait_recv()
        for t in part:
            near = ask_ref[1, t : t + 1, :] < 3 * CELLS
            up_out[t] = jnp.where(near, up_out[t].astype(F32), corner_in[t].astype(F32)).astype(BF)
        at = pl.ds(part.start, len(part))
        ups.append(remote(up_out.at[at], up_in.at[at], up_send.at[j], up_recv.at[j], other(1, 0)))
    for t in range(n_tiles):
        fa_ref[t] = feat_ref[tf_ref[t]]
        fb_ref[t] = feat_ref[lax.rem(ts_ref[t], CELLS)]
    sides.wait_recv()
    for t in range(n_tiles):
        own = mine[t : t + 1, :] < CELLS
        fb_ref[t] = jnp.where(own, fb_ref[t].astype(F32), side_in[t].astype(F32)).astype(BF)
    for j in range(GROUPS):
        ups[j].wait_recv()
        for t in range(j * n_tiles // GROUPS, (j + 1) * n_tiles // GROUPS):
            near = mine[t : t + 1, :] < 2 * CELLS
            fb_ref[t] = jnp.where(near, fb_ref[t].astype(F32), up_in[t].astype(F32)).astype(BF)
    for copy in sent:
        copy.wait()
    for copy in asks + corners + [sides] + ups:
        copy.wait_send()


def tile_kernel(
    tf_ref, ts_ref, ca_ref, cb_ref, pos_ref, gotpos_ref, fa_ref, fb_ref, wa_ref, wb_ref, wr_ref, mix_ref, ow_ref,
    own_ref, gb_ref,
    xb_ref, mixt_ref, owb_ref, lead, projc, d_ref, r2_ref, diff_ref, h_s, h2_s, y_s, slope_s, z_s,
):
    W = ROWS * CELL
    PW = PIECE * CELL
    tiles = gb_ref.shape[0]

    for t in range(tiles):
        slots = cell_slots(lax.rem(ts_ref[t], CELLS))
        source = ts_ref[t] // CELLS
        came = gotpos_ref[jnp.maximum(source - 1, 0), :, slots].astype(F32)
        xb_ref[t] = jnp.where(source == 0, pos_ref[:, slots].astype(F32), came)
    mixt_ref[...] = (mix_ref[...].astype(F32).T * 0.5).astype(BF)
    owb_ref[...] = jnp.broadcast_to(ow_ref[...], (CELL, LAT)).T
    own_ref[...] = jnp.zeros_like(own_ref)

    def prepare(t):
        swap = cb_ref[t] < ca_ref[t]
        slots = cell_slots(tf_ref[t])
        proj_a = dot(fa_ref[t], wa_ref[...], ((1,), (0,))).astype(BF).astype(F32)
        proj_b = dot(fb_ref[t], wb_ref[...], ((1,), (0,))).astype(BF).astype(F32)
        pr = jnp.where(swap, proj_b, proj_a) * 0.5
        pc = jnp.where(swap, proj_a, proj_b) * 0.5
        projc[t] = pc.T
        groups = pr.reshape(CELL // SUB, SUB, LAT)
        lead[t] = jnp.concatenate([groups, jnp.zeros_like(groups)], axis=1).astype(BF)
        xa = pos_ref[:, slots].astype(F32)
        xb = xb_ref[t]
        xr = jnp.where(swap, xb, xa)
        xc = jnp.where(swap, xa, xb)
        r2 = jnp.zeros((CELL, CELL), F32)
        for k in range(3):
            d = jnp.broadcast_to(xr[k : k + 1], (CELL, CELL)).T - jnp.broadcast_to(xc[k : k + 1], (CELL, CELL))
            diff_ref[t, k] = d
            r2 = r2 + d * d
        r2_ref[t] = r2 * SPREAD

    def prepare_two(u, _):
        prepare(2 * u)
        prepare(2 * u + 1)
        return 0

    lax.fori_loop(0, tiles // 2, prepare_two, 0)

    hot = lax.broadcasted_iota(jnp.int32, (16, SUB * CELL), 0)
    hot = hot == lax.broadcasted_iota(jnp.int32, (16, SUB * CELL), 1) // CELL
    hot = hot.astype(F32).astype(BF)
    centers = lax.broadcasted_iota(jnp.int32, (NB, CELL), 0).astype(F32) * (STEP * SPREAD)
    n_sub = ROWS // SUB
    per_sub = SUB // PIECE

    def subs_of(t):
        return (jnp.minimum(ca_ref[t], cb_ref[t]) + SUB - 1) // SUB

    def following(place):
        places = []
        for _ in range(n_sub):
            t, c = place
            last = c + 1 >= subs_of(jnp.minimum(t, tiles - 1))
            place = jnp.where(last, jnp.minimum(t + 1, tiles), t), jnp.where(last, 0, c + 1)
            places.append(place)
        return tuple(places)

    def step(it, carry):
        at1, at2, at3, at4 = carry
        rows = lambda c: pl.ds(pl.multiple_of(c * SUB, SUB), SUB)
        slope_at = lax.rem(it, 2)
        z_at = lax.rem(it, 3)
        owb = jnp.concatenate([owb_ref[...]] * PIECE, axis=1)
        for p in range(ROWS // PIECE):
            cs = slice(p * PW, (p + 1) * PW)
            q = p % per_sub
            if q == 0:
                (t1, c1), (t2, _), (t3, c3), (t4, c4) = (at[p // per_sub] for at in carry)
                in1 = jnp.minimum(t1, tiles - 1)
                r2 = r2_ref[in1, rows(c1), :]
                lhs = jnp.concatenate([wr_ref[...] * jnp.asarray(0.5, BF), lead[in1, c1]], axis=0)
                pc = jnp.concatenate([projc[jnp.minimum(t2, tiles - 1)]] * PIECE, axis=1)
                cores = []
                readouts = []
            ds = (y_s[:, cs] * slope_s[slope_at, :, cs]).astype(BF)
            z = z_s[z_at, :, cs]
            h2 = h2_s[:, cs]
            tt = jnp.tanh(h2)
            v = owb * (1 + tt)
            act = h2 * v
            ro = jnp.sum(act, axis=0, keepdims=True)
            back = (v + act * (1 - tt)).astype(BF)
            h = h_s[:, cs] + pc
            tt = jnp.tanh(h)
            v = 1 + tt
            act = h * v
            slope_s[slope_at, :, cs] = v + act * (1 - tt)
            latent = act.astype(BF)
            gs = []
            zs = []
            for i in range(q * PIECE, (q + 1) * PIECE):
                o = jnp.broadcast_to(r2[i : i + 1], (NB, CELL)) - centers
                g = jnp.exp2(-(o * o))
                gs.append(g.astype(BF))
                zs.append(g * o)
            z_s[z_at, :, cs] = jnp.concatenate(zs, axis=1)
            rhs = jnp.concatenate([jnp.concatenate(gs, axis=1), hot[:, q * PW : (q + 1) * PW]], axis=0)
            y_s[:, cs] = dot(mix_ref[...], back, ((1,), (0,)))
            h_s[:, cs] = dot(lhs, rhs, ((0,), (0,)))
            z = dot(wr_ref[...], ds, ((1,), (0,))) * z
            h2_s[:, cs] = dot(mixt_ref[...], latent, ((1,), (0,)))
            for i in range(PIECE):
                cores.append(jnp.sum(z[:, i * CELL : (i + 1) * CELL], axis=0, keepdims=True))
                readouts.append(ro[:, i * CELL : (i + 1) * CELL])
            if q == per_sub - 1:
                d_ref[0, t4, rows(c4), :] = jnp.concatenate(cores, axis=0)
                d_ref[1, t3, rows(c3), :] = jnp.concatenate(readouts, axis=0)
        return following(at1[-1]), at1, at2, at3

    total = jnp.int32(0)
    for t in range(tiles):
        total = total + subs_of(t)
    zero = jnp.int32(0)
    start = (zero, zero)
    start = ((start,) + following(start))[:n_sub]
    idle = ((jnp.int32(tiles), zero),) * n_sub
    lax.fori_loop(0, (total + n_sub - 1) // n_sub + 3, step, (start, idle, idle, idle))

    def finish(t):
        ca, cb = ca_ref[t], cb_ref[t]
        swap = cb < ca
        row = lax.broadcasted_iota(jnp.int32, (CELL, CELL), 0)
        col = lax.broadcasted_iota(jnp.int32, (CELL, CELL), 1)
        live = (row < jnp.minimum(ca, cb)) & (col < jnp.maximum(ca, cb))
        env = 1 - r2_ref[t] * (0.125 / SPREAD)
        dd = env * env * (d_ref[0, t] * (-4.0 / (SPREAD * 4 * CELL))) + env * (d_ref[1, t] * (-0.25 / CELL))
        dd = jnp.where(live, 2 * dd, 0.0)
        gr = []
        gc = []
        for k in range(3):
            pull = diff_ref[t, k] * dd
            gr.append(jnp.sum(pull.T, axis=0, keepdims=True))
            gc.append(-jnp.sum(pull, axis=0, keepdims=True))
        gr = jnp.concatenate(gr, axis=0)
        gc = jnp.concatenate(gc, axis=0)
        return jnp.where(swap, gc, gr), jnp.where(swap, gr, gc)

    def put(t, ga, gb):
        own_ref[:, cell_slots(tf_ref[t])] -= ga
        gb_ref[t] = gb

        @pl.when(ts_ref[t] // CELLS == 0)
        def _():
            own_ref[:, cell_slots(lax.rem(ts_ref[t], CELLS))] -= gb

    def finish_two(u, _):
        one = finish(2 * u)
        two = finish(2 * u + 1)
        put(2 * u, *one)
        put(2 * u + 1, *two)
        return 0

    lax.fori_loop(0, tiles // 2, finish_two, 0)


def return_kernel(n_tiles, ask_ref, own_ref, second_ref, out_ref, back_ref, send_sem, recv_sem):
    barrier = pltpu.get_barrier_semaphore()
    for g, d in WAYS:
        pl.semaphore_signal(barrier, inc=1, device_id=other(g, d), device_id_type=MESH)
    pl.semaphore_wait(barrier, len(WAYS))
    copies = []
    for w, (g, d) in enumerate(WAYS):
        copy = pltpu.make_async_remote_copy(
            src_ref=second_ref, dst_ref=back_ref.at[w], send_sem=send_sem.at[w], recv_sem=recv_sem.at[w],
            device_id=other(-g, -d), device_id_type=MESH,
        )
        copy.start()
        copies.append(copy)
    for copy in copies:
        copy.wait()

    def one(c, _):
        slots = cell_slots(c)
        total = own_ref[:, slots]
        for w in range(len(WAYS)):
            for t in range(n_tiles):
                total -= jnp.where(ask_ref[w, t : t + 1, :] == (w + 1) * CELLS + c, back_ref[w, t], 0.0)
        out_ref[:, slots] = total
        return 0

    lax.fori_loop(0, CELLS, one, 0)


def on_device(
    positions, features, tile_first, tile_second, count_first, count_second, w_first, w_second, radial_weight,
    mix_weight, out_weight,
):
    tiles = tile_first.shape[0]
    smem = pl.BlockSpec(memory_space=pltpu.SMEM)
    vmem = pl.BlockSpec(memory_space=pltpu.VMEM)

    anywhere = pl.BlockSpec(memory_space=pl.ANY)
    dma = pltpu.SemaphoreType.DMA
    n = len(WAYS)
    cells = (tiles, CELL, LAT)
    ask, first, second, got_pos = pl.pallas_call(
        functools.partial(fetch_kernel, tiles),
        out_shape=[
            jax.ShapeDtypeStruct((n, tiles, CELL), jnp.int32),
            jax.ShapeDtypeStruct(cells, BF),
            jax.ShapeDtypeStruct(cells, BF),
            jax.ShapeDtypeStruct((n, *positions.shape), BF),
        ],
        in_specs=[smem, smem, anywhere, anywhere],
        out_specs=[vmem, vmem, vmem, anywhere],
        scratch_shapes=[
            pltpu.VMEM((CELLS, CELL, LAT), BF),
            dma(()),
            pltpu.VMEM((tiles, CELL), jnp.int32),
            pltpu.SMEM((n, tiles, CELL), jnp.int32),
        ]
        + [pltpu.VMEM(cells, BF)] * 6
        + [dma((n,))] * 3
        + [dma((GROUPS,))] * 4
        + [dma(())] * 2
        + [dma((n,))] * 2,
        compiler_params=pltpu.CompilerParams(collective_id=0, has_side_effects=True),
        name="fetch",
    )(tile_first, tile_second, positions, features.reshape(-1, CELL, LAT))
    W = ROWS * CELL
    own, partial = pl.pallas_call(
        tile_kernel,
        out_shape=[jax.ShapeDtypeStruct(positions.shape, F32), jax.ShapeDtypeStruct((tiles, 3, CELL), F32)],
        in_specs=[smem] * 4 + [vmem] * 9,
        out_specs=[vmem] * 2,
        scratch_shapes=[
            pltpu.VMEM((tiles, 3, CELL), F32),
            pltpu.VMEM((LAT, LAT), BF),
            pltpu.VMEM((LAT, CELL), F32),
            pltpu.VMEM((tiles, CELL // SUB, 16, LAT), BF),
            pltpu.VMEM((tiles, LAT, CELL), F32),
            pltpu.VMEM((2, tiles + 1, CELL, CELL), F32),
            pltpu.VMEM((tiles, CELL, CELL), F32),
            pltpu.VMEM((tiles, 3, CELL, CELL), F32),
            pltpu.VMEM((LAT, W), F32),
            pltpu.VMEM((LAT, W), F32),
            pltpu.VMEM((LAT, W), F32),
            pltpu.VMEM((2, LAT, W), F32),
            pltpu.VMEM((3, NB, W), F32),
        ],
        compiler_params=pltpu.CompilerParams(vmem_limit_bytes=60 << 20),
        name="tiles",
    )(
        tile_first, tile_second, count_first, count_second, positions, got_pos, first, second, w_first, w_second,
        radial_weight, mix_weight, out_weight.reshape(1, LAT),
    )
    return pl.pallas_call(
        functools.partial(return_kernel, tiles),
        out_shape=jax.ShapeDtypeStruct(positions.shape, F32),
        in_specs=[vmem] * 3,
        out_specs=vmem,
        scratch_shapes=[pltpu.VMEM((n, tiles, 3, CELL), F32), dma((n,)), dma((n,))],
        compiler_params=pltpu.CompilerParams(collective_id=1, has_side_effects=True),
        name="return",
    )(ask, own, partial)


def solution(mesh):
    each = P(("grp", "dev"))
    in_specs = (P(None, ("grp", "dev")), P(("grp", "dev"), None), each, each, each, each, P(), P(), P(), P(), P())
    return jax.shard_map(
        on_device, mesh=mesh, in_specs=in_specs, out_specs=P(None, ("grp", "dev")), check_vma=False
    )
```

```python
import functools

import jax
import jax.numpy as jnp
from jax import lax
from jax.experimental import pallas as pl
from jax.experimental.pallas import tpu as pltpu
from jax.sharding import PartitionSpec as P

CELL = 128
CELLS = 32
LAT = 128
NB = 16
ROWS = 24
SUB = 8
PIECE = 2
GROUPS = 4
WAYS = ((0, 1), (1, 0), (1, 1))
MESH = pl.DeviceIdType.MESH
SPREAD = 2.8853900817779268**0.5
STEP = 6.75 / NB
F32 = jnp.float32
BF = jnp.bfloat16


def dot(a, b, dims):
    return lax.dot_general(a, b, (dims, ((), ())), preferred_element_type=F32)


def cell_slots(cell):
    return pl.ds(pl.multiple_of(cell * CELL, CELL), CELL)


def other(by_grp, by_dev):
    g = lax.axis_index("grp") + by_grp
    d = lax.axis_index("dev") + by_dev
    n_grp = lax.axis_size("grp")
    n_dev = lax.axis_size("dev")
    return lax.rem(g + n_grp, n_grp), lax.rem(d + n_dev, n_dev)


def remote(src, dst, send, recv, to):
    copy = pltpu.make_async_remote_copy(
        src_ref=src, dst_ref=dst, send_sem=send, recv_sem=recv, device_id=to, device_id_type=MESH
    )
    copy.start()
    return copy


def fetch_kernel(
    n_tiles, tf_ref, ts_ref, pos_any, feat_any, ask_ref, fa_ref, fb_ref, gotpos_ref,
    feat_ref, feat_sem, mine, numbers, corner_out, corner_in, side_out, side_in, up_out, up_in,
    ask_send, ask_recv, local_sem, corner_send, corner_recv, up_send, up_recv, side_send, side_recv, pos_send, pos_recv,
):
    features = pltpu.make_async_copy(feat_any, feat_ref, feat_sem)
    features.start()
    barrier = pltpu.get_barrier_semaphore()
    for g, d in WAYS:
        pl.semaphore_signal(barrier, inc=1, device_id=other(g, d), device_id_type=MESH)
        pl.semaphore_signal(barrier, inc=1, device_id=other(-g, -d), device_id_type=MESH)
    for t in range(n_tiles):
        mine[t : t + 1, :] = jnp.full((1, CELL), ts_ref[t], jnp.int32)
    pl.semaphore_wait(barrier, 2 * len(WAYS))

    asks = [
        remote(mine, ask_ref.at[w], ask_send.at[w], ask_recv.at[w], other(-g, -d)) for w, (g, d) in enumerate(WAYS)
    ]
    sent = [
        remote(pos_any, gotpos_ref.at[w], pos_send.at[w], pos_recv.at[w], other(g, d)) for w, (g, d) in enumerate(WAYS)
    ]
    features.wait()

    def hear(w):
        asks[w].wait_recv()
        local = pltpu.make_async_copy(ask_ref.at[w], numbers.at[w], local_sem.at[w])
        local.start()
        local.wait()

    def pick(w, t):
        return feat_ref[lax.rem(numbers[w, t, 0], CELLS)]

    hear(2)
    corners = []
    for j in range(GROUPS):
        part = range(j * n_tiles // GROUPS, (j + 1) * n_tiles // GROUPS)
        for t in part:
            corner_out[t] = pick(2, t)
        at = pl.ds(part.start, len(part))
        corners.append(
            remote(corner_out.at[at], corner_in.at[at], corner_send.at[j], corner_recv.at[j], other(0, 1))
        )
    hear(0)
    for t in range(n_tiles):
        side_out[t] = pick(0, t)
    sides = remote(side_out, side_in, side_send, side_recv, other(0, 1))
    hear(1)
    for t in range(n_tiles):
        up_out[t] = pick(1, t)
    ups = []
    for j in range(GROUPS):
        part = range(j * n_tiles // GROUPS, (j + 1) * n_tiles // GROUPS)
        corners[j].wait_recv()
        for t in part:
            near = ask_ref[1, t : t + 1, :] < 3 * CELLS
            up_out[t] = jnp.where(near, up_out[t].astype(F32), corner_in[t].astype(F32)).astype(BF)
        at = pl.ds(part.start, len(part))
        ups.append(remote(up_out.at[at], up_in.at[at], up_send.at[j], up_recv.at[j], other(1, 0)))
    for t in range(n_tiles):
        fa_ref[t] = feat_ref[tf_ref[t]]
        fb_ref[t] = feat_ref[lax.rem(ts_ref[t], CELLS)]
    sides.wait_recv()
    for t in range(n_tiles):
        own = mine[t : t + 1, :] < CELLS
        fb_ref[t] = jnp.where(own, fb_ref[t].astype(F32), side_in[t].astype(F32)).astype(BF)
    for j in range(GROUPS):
        ups[j].wait_recv()
        for t in range(j * n_tiles // GROUPS, (j + 1) * n_tiles // GROUPS):
            near = mine[t : t + 1, :] < 2 * CELLS
            fb_ref[t] = jnp.where(near, fb_ref[t].astype(F32), up_in[t].astype(F32)).astype(BF)
    for copy in sent:
        copy.wait()
    for copy in asks + corners + [sides] + ups:
        copy.wait_send()


def tile_kernel(
    tf_ref, ts_ref, ca_ref, cb_ref, pos_ref, gotpos_ref, fa_ref, fb_ref, wa_ref, wb_ref, wr_ref, mix_ref, ow_ref,
    own_ref, gb_ref,
    xb_ref, mixt_ref, owb_ref, lead, projc, d_ref, r2_ref, diff_ref, h_s, h2_s, y_s, slope_s, z_s,
):
    W = ROWS * CELL
    PW = PIECE * CELL
    tiles = gb_ref.shape[0]

    for t in range(tiles):
        slots = cell_slots(lax.rem(ts_ref[t], CELLS))
        source = ts_ref[t] // CELLS
        came = gotpos_ref[jnp.maximum(source - 1, 0), :, slots].astype(F32)
        xb_ref[t] = jnp.where(source == 0, pos_ref[:, slots].astype(F32), came)
    mixt_ref[...] = (mix_ref[...].astype(F32).T * 0.5).astype(BF)
    owb_ref[...] = jnp.broadcast_to(ow_ref[...], (CELL, LAT)).T
    own_ref[...] = jnp.zeros_like(own_ref)

    def prepare(t):
        swap = cb_ref[t] < ca_ref[t]
        slots = cell_slots(tf_ref[t])
        proj_a = dot(fa_ref[t], wa_ref[...], ((1,), (0,))).astype(BF).astype(F32)
        proj_b = dot(fb_ref[t], wb_ref[...], ((1,), (0,))).astype(BF).astype(F32)
        pr = jnp.where(swap, proj_b, proj_a) * 0.5
        pc = jnp.where(swap, proj_a, proj_b) * 0.5
        projc[t] = pc.T
        groups = pr.reshape(CELL // SUB, SUB, LAT)
        lead[t] = jnp.concatenate([groups, jnp.zeros_like(groups)], axis=1).astype(BF)
        xa = pos_ref[:, slots].astype(F32)
        xb = xb_ref[t]
        xr = jnp.where(swap, xb, xa)
        xc = jnp.where(swap, xa, xb)
        r2 = jnp.zeros((CELL, CELL), F32)
        for k in range(3):
            d = jnp.broadcast_to(xr[k : k + 1], (CELL, CELL)).T - jnp.broadcast_to(xc[k : k + 1], (CELL, CELL))
            diff_ref[t, k] = d
            r2 = r2 + d * d
        r2_ref[t] = r2 * SPREAD

    def prepare_two(u, _):
        prepare(2 * u)
        prepare(2 * u + 1)
        return 0

    lax.fori_loop(0, tiles // 2, prepare_two, 0)

    hot = lax.broadcasted_iota(jnp.int32, (16, SUB * CELL), 0)
    hot = hot == lax.broadcasted_iota(jnp.int32, (16, SUB * CELL), 1) // CELL
    hot = hot.astype(F32).astype(BF)
    centers = lax.broadcasted_iota(jnp.int32, (NB, CELL), 0).astype(F32) * (STEP * SPREAD)
    n_sub = ROWS // SUB
    per_sub = SUB // PIECE

    def subs_of(t):
        return (jnp.minimum(ca_ref[t], cb_ref[t]) + SUB - 1) // SUB

    def following(place):
        places = []
        for _ in range(n_sub):
            t, c = place
            last = c + 1 >= subs_of(jnp.minimum(t, tiles - 1))
            place = jnp.where(last, jnp.minimum(t + 1, tiles), t), jnp.where(last, 0, c + 1)
            places.append(place)
        return tuple(places)

    def step(it, carry):
        at1, at2, at3, at4 = carry
        rows = lambda c: pl.ds(pl.multiple_of(c * SUB, SUB), SUB)
        slope_at = lax.rem(it, 2)
        z_at = lax.rem(it, 3)
        owb = jnp.concatenate([owb_ref[...]] * PIECE, axis=1)
        for p in range(ROWS // PIECE):
            cs = slice(p * PW, (p + 1) * PW)
            q = p % per_sub
            if q == 0:
                (t1, c1), (t2, _), (t3, c3), (t4, c4) = (at[p // per_sub] for at in carry)
                in1 = jnp.minimum(t1, tiles - 1)
                r2 = r2_ref[in1, rows(c1), :]
                lhs = jnp.concatenate([wr_ref[...] * jnp.asarray(0.5, BF), lead[in1, c1]], axis=0)
                pc = jnp.concatenate([projc[jnp.minimum(t2, tiles - 1)]] * PIECE, axis=1)
                cores = []
                readouts = []
            ds = (y_s[:, cs] * slope_s[slope_at, :, cs]).astype(BF)
            z = z_s[z_at, :, cs]
            h2 = h2_s[:, cs]
            tt = jnp.tanh(h2)
            v = owb * (1 + tt)
            act = h2 * v
            ro = jnp.sum(act, axis=0, keepdims=True)
            back = (v + act * (1 - tt)).astype(BF)
            h = h_s[:, cs] + pc
            tt = jnp.tanh(h)
            v = 1 + tt
            act = h * v
            slope_s[slope_at, :, cs] = v + act * (1 - tt)
            latent = act.astype(BF)
            gs = []
            zs = []
            for i in range(q * PIECE, (q + 1) * PIECE):
                o = jnp.broadcast_to(r2[i : i + 1], (NB, CELL)) - centers
                g = jnp.exp2(-(o * o))
                gs.append(g.astype(BF))
                zs.append(g * o)
            z_s[z_at, :, cs] = jnp.concatenate(zs, axis=1)
            rhs = jnp.concatenate([jnp.concatenate(gs, axis=1), hot[:, q * PW : (q + 1) * PW]], axis=0)
            y_s[:, cs] = dot(mix_ref[...], back, ((1,), (0,)))
            h_s[:, cs] = dot(lhs, rhs, ((0,), (0,)))
            z = dot(wr_ref[...], ds, ((1,), (0,))) * z
            h2_s[:, cs] = dot(mixt_ref[...], latent, ((1,), (0,)))
            for i in range(PIECE):
                cores.append(jnp.sum(z[:, i * CELL : (i + 1) * CELL], axis=0, keepdims=True))
                readouts.append(ro[:, i * CELL : (i + 1) * CELL])
            if q == per_sub - 1:
                d_ref[0, t4, rows(c4), :] = jnp.concatenate(cores, axis=0)
                d_ref[1, t3, rows(c3), :] = jnp.concatenate(readouts, axis=0)
        return following(at1[-1]), at1, at2, at3

    total = jnp.int32(0)
    for t in range(tiles):
        total = total + subs_of(t)
    zero = jnp.int32(0)
    start = (zero, zero)
    start = ((start,) + following(start))[:n_sub]
    idle = ((jnp.int32(tiles), zero),) * n_sub
    lax.fori_loop(0, (total + n_sub - 1) // n_sub + 3, step, (start, idle, idle, idle))

    def finish(t):
        ca, cb = ca_ref[t], cb_ref[t]
        swap = cb < ca
        row = lax.broadcasted_iota(jnp.int32, (CELL, CELL), 0)
        col = lax.broadcasted_iota(jnp.int32, (CELL, CELL), 1)
        live = (row < jnp.minimum(ca, cb)) & (col < jnp.maximum(ca, cb))
        env = 1 - r2_ref[t] * (0.125 / SPREAD)
        dd = env * env * (d_ref[0, t] * (-4.0 / (SPREAD * 4 * CELL))) + env * (d_ref[1, t] * (-0.25 / CELL))
        dd = jnp.where(live, 2 * dd, 0.0)
        gr = []
        gc = []
        for k in range(3):
            pull = diff_ref[t, k] * dd
            gr.append(jnp.sum(pull.T, axis=0, keepdims=True))
            gc.append(-jnp.sum(pull, axis=0, keepdims=True))
        gr = jnp.concatenate(gr, axis=0)
        gc = jnp.concatenate(gc, axis=0)
        return jnp.where(swap, gc, gr), jnp.where(swap, gr, gc)

    def put(t, ga, gb):
        own_ref[:, cell_slots(tf_ref[t])] -= ga
        gb_ref[t] = gb

        @pl.when(ts_ref[t] // CELLS == 0)
        def _():
            own_ref[:, cell_slots(lax.rem(ts_ref[t], CELLS))] -= gb

    def finish_two(u, _):
        one = finish(2 * u)
        two = finish(2 * u + 1)
        put(2 * u, *one)
        put(2 * u + 1, *two)
        return 0

    lax.fori_loop(0, tiles // 2, finish_two, 0)


def return_kernel(n_tiles, ask_ref, own_ref, second_ref, out_ref, back_ref, send_sem, recv_sem):
    barrier = pltpu.get_barrier_semaphore()
    for g, d in WAYS:
        pl.semaphore_signal(barrier, inc=1, device_id=other(g, d), device_id_type=MESH)
    pl.semaphore_wait(barrier, len(WAYS))
    copies = []
    for w, (g, d) in enumerate(WAYS):
        copy = pltpu.make_async_remote_copy(
            src_ref=second_ref, dst_ref=back_ref.at[w], send_sem=send_sem.at[w], recv_sem=recv_sem.at[w],
            device_id=other(-g, -d), device_id_type=MESH,
        )
        copy.start()
        copies.append(copy)
    for copy in copies:
        copy.wait()

    asked = [[ask_ref[w, t : t + 1, :] - (w + 1) * CELLS for t in range(n_tiles)] for w in range(len(WAYS))]

    def four(u, _):
        for i in range(4):
            c = 4 * u + i
            sums = []
            for w in range(len(WAYS)):
                hits = [jnp.where(asked[w][t] == c, back_ref[w, t], 0.0) for t in range(n_tiles)]
                while len(hits) > 1:
                    hits = [x + y for x, y in zip(hits[::2], hits[1::2], strict=True)]
                sums += hits
            slots = cell_slots(c)
            out_ref[:, slots] = own_ref[:, slots] - (sums[0] + sums[1] + sums[2])
        return 0

    lax.fori_loop(0, CELLS // 4, four, 0)


def on_device(
    positions, features, tile_first, tile_second, count_first, count_second, w_first, w_second, radial_weight,
    mix_weight, out_weight,
):
    tiles = tile_first.shape[0]
    smem = pl.BlockSpec(memory_space=pltpu.SMEM)
    vmem = pl.BlockSpec(memory_space=pltpu.VMEM)

    anywhere = pl.BlockSpec(memory_space=pl.ANY)
    dma = pltpu.SemaphoreType.DMA
    n = len(WAYS)
    cells = (tiles, CELL, LAT)
    ask, first, second, got_pos = pl.pallas_call(
        functools.partial(fetch_kernel, tiles),
        out_shape=[
            jax.ShapeDtypeStruct((n, tiles, CELL), jnp.int32),
            jax.ShapeDtypeStruct(cells, BF),
            jax.ShapeDtypeStruct(cells, BF),
            jax.ShapeDtypeStruct((n, *positions.shape), BF),
        ],
        in_specs=[smem, smem, anywhere, anywhere],
        out_specs=[vmem, vmem, vmem, anywhere],
        scratch_shapes=[
            pltpu.VMEM((CELLS, CELL, LAT), BF),
            dma(()),
            pltpu.VMEM((tiles, CELL), jnp.int32),
            pltpu.SMEM((n, tiles, CELL), jnp.int32),
        ]
        + [pltpu.VMEM(cells, BF)] * 6
        + [dma((n,))] * 3
        + [dma((GROUPS,))] * 4
        + [dma(())] * 2
        + [dma((n,))] * 2,
        compiler_params=pltpu.CompilerParams(collective_id=0, has_side_effects=True),
        name="fetch",
    )(tile_first, tile_second, positions, features.reshape(-1, CELL, LAT))
    W = ROWS * CELL
    own, partial = pl.pallas_call(
        tile_kernel,
        out_shape=[jax.ShapeDtypeStruct(positions.shape, F32), jax.ShapeDtypeStruct((tiles, 3, CELL), F32)],
        in_specs=[smem] * 4 + [vmem] * 9,
        out_specs=[vmem] * 2,
        scratch_shapes=[
            pltpu.VMEM((tiles, 3, CELL), F32),
            pltpu.VMEM((LAT, LAT), BF),
            pltpu.VMEM((LAT, CELL), F32),
            pltpu.VMEM((tiles, CELL // SUB, 16, LAT), BF),
            pltpu.VMEM((tiles, LAT, CELL), F32),
            pltpu.VMEM((2, tiles + 1, CELL, CELL), F32),
            pltpu.VMEM((tiles, CELL, CELL), F32),
            pltpu.VMEM((tiles, 3, CELL, CELL), F32),
            pltpu.VMEM((LAT, W), F32),
            pltpu.VMEM((LAT, W), F32),
            pltpu.VMEM((LAT, W), F32),
            pltpu.VMEM((2, LAT, W), F32),
            pltpu.VMEM((3, NB, W), F32),
        ],
        compiler_params=pltpu.CompilerParams(vmem_limit_bytes=60 << 20),
        name="tiles",
    )(
        tile_first, tile_second, count_first, count_second, positions, got_pos, first, second, w_first, w_second,
        radial_weight, mix_weight, out_weight.reshape(1, LAT),
    )
    return pl.pallas_call(
        functools.partial(return_kernel, tiles),
        out_shape=jax.ShapeDtypeStruct(positions.shape, F32),
        in_specs=[vmem] * 3,
        out_specs=vmem,
        scratch_shapes=[pltpu.VMEM((n, tiles, 3, CELL), F32), dma((n,)), dma((n,))],
        compiler_params=pltpu.CompilerParams(collective_id=1, has_side_effects=True),
        name="return",
    )(ask, own, partial)


def solution(mesh):
    each = P(("grp", "dev"))
    in_specs = (P(None, ("grp", "dev")), P(("grp", "dev"), None), each, each, each, each, P(), P(), P(), P(), P())
    return jax.shard_map(
        on_device, mesh=mesh, in_specs=in_specs, out_specs=P(None, ("grp", "dev")), check_vma=False
    )
```

```python
import functools

import jax
import jax.numpy as jnp
from jax import lax
from jax.experimental import pallas as pl
from jax.experimental.pallas import tpu as pltpu
from jax.sharding import PartitionSpec as P

CELL = 128
CELLS = 32
LAT = 128
NB = 16
ROWS = 24
SUB = 8
PIECE = 2
GROUPS = 4
WAYS = ((0, 1), (1, 0), (1, 1))
MESH = pl.DeviceIdType.MESH
SPREAD = 2.8853900817779268**0.5
STEP = 6.75 / NB
F32 = jnp.float32
BF = jnp.bfloat16


def dot(a, b, dims):
    return lax.dot_general(a, b, (dims, ((), ())), preferred_element_type=F32)


def cell_slots(cell):
    return pl.ds(pl.multiple_of(cell * CELL, CELL), CELL)


def other(by_grp, by_dev):
    g = lax.axis_index("grp") + by_grp
    d = lax.axis_index("dev") + by_dev
    n_grp = lax.axis_size("grp")
    n_dev = lax.axis_size("dev")
    return lax.rem(g + n_grp, n_grp), lax.rem(d + n_dev, n_dev)


def remote(src, dst, send, recv, to):
    copy = pltpu.make_async_remote_copy(
        src_ref=src, dst_ref=dst, send_sem=send, recv_sem=recv, device_id=to, device_id_type=MESH
    )
    copy.start()
    return copy


def fetch_kernel(
    n_tiles, tf_ref, ts_ref, pos_any, feat_any, ask_ref, fa_ref, fb_ref, gotpos_ref,
    feat_ref, feat_sem, mine, numbers, corner_out, corner_in, side_out, side_in, up_out, up_in,
    ask_send, ask_recv, local_sem, corner_send, corner_recv, up_send, up_recv, side_send, side_recv, pos_send, pos_recv,
):
    features = pltpu.make_async_copy(feat_any, feat_ref, feat_sem)
    features.start()
    barrier = pltpu.get_barrier_semaphore()
    for g, d in WAYS:
        pl.semaphore_signal(barrier, inc=1, device_id=other(g, d), device_id_type=MESH)
        pl.semaphore_signal(barrier, inc=1, device_id=other(-g, -d), device_id_type=MESH)
    for t in range(n_tiles):
        mine[t : t + 1, :] = jnp.full((1, CELL), ts_ref[t], jnp.int32)
    pl.semaphore_wait(barrier, 2 * len(WAYS))

    asks = {}
    for w in (2, 0, 1):
        g, d = WAYS[w]
        asks[w] = remote(mine, ask_ref.at[w], ask_send.at[w], ask_recv.at[w], other(-g, -d))
    sent = [
        remote(pos_any, gotpos_ref.at[w], pos_send.at[w], pos_recv.at[w], other(g, d)) for w, (g, d) in enumerate(WAYS)
    ]
    features.wait()

    def hear(w):
        asks[w].wait_recv()
        local = pltpu.make_async_copy(ask_ref.at[w], numbers.at[w], local_sem.at[w])
        local.start()
        local.wait()

    def pick(w, t):
        return feat_ref[lax.rem(numbers[w, t, 0], CELLS)]

    hear(2)
    corners = []
    for j in range(GROUPS):
        part = range(j * n_tiles // GROUPS, (j + 1) * n_tiles // GROUPS)
        for t in part:
            corner_out[t] = pick(2, t)
        at = pl.ds(part.start, len(part))
        corners.append(
            remote(corner_out.at[at], corner_in.at[at], corner_send.at[j], corner_recv.at[j], other(0, 1))
        )
    hear(0)
    for t in range(n_tiles):
        side_out[t] = pick(0, t)
    sides = remote(side_out, side_in, side_send, side_recv, other(0, 1))
    hear(1)
    for t in range(n_tiles):
        up_out[t] = pick(1, t)
    ups = []
    for j in range(GROUPS):
        part = range(j * n_tiles // GROUPS, (j + 1) * n_tiles // GROUPS)
        corners[j].wait_recv()
        for t in part:
            near = ask_ref[1, t : t + 1, :] < 3 * CELLS
            up_out[t] = jnp.where(near, up_out[t].astype(F32), corner_in[t].astype(F32)).astype(BF)
        at = pl.ds(part.start, len(part))
        ups.append(remote(up_out.at[at], up_in.at[at], up_send.at[j], up_recv.at[j], other(1, 0)))
    for t in range(n_tiles):
        fa_ref[t] = feat_ref[tf_ref[t]]
        fb_ref[t] = feat_ref[lax.rem(ts_ref[t], CELLS)]
    sides.wait_recv()
    for t in range(n_tiles):
        own = mine[t : t + 1, :] < CELLS
        fb_ref[t] = jnp.where(own, fb_ref[t].astype(F32), side_in[t].astype(F32)).astype(BF)
    for j in range(GROUPS):
        ups[j].wait_recv()
        for t in range(j * n_tiles // GROUPS, (j + 1) * n_tiles // GROUPS):
            near = mine[t : t + 1, :] < 2 * CELLS
            fb_ref[t] = jnp.where(near, fb_ref[t].astype(F32), up_in[t].astype(F32)).astype(BF)
    for copy in sent:
        copy.wait()
    for copy in list(asks.values()) + corners + [sides] + ups:
        copy.wait_send()


def tile_kernel(
    tf_ref, ts_ref, ca_ref, cb_ref, pos_ref, gotpos_ref, fa_ref, fb_ref, wa_ref, wb_ref, wr_ref, mix_ref, ow_ref,
    own_ref, gb_ref,
    xb_ref, mixt_ref, owb_ref, lead, projc, d_ref, r2_ref, diff_ref, h_s, h2_s, y_s, slope_s, z_s,
):
    W = ROWS * CELL
    PW = PIECE * CELL
    tiles = gb_ref.shape[0]

    for t in range(tiles):
        slots = cell_slots(lax.rem(ts_ref[t], CELLS))
        source = ts_ref[t] // CELLS
        came = gotpos_ref[jnp.maximum(source - 1, 0), :, slots].astype(F32)
        xb_ref[t] = jnp.where(source == 0, pos_ref[:, slots].astype(F32), came)
    mixt_ref[...] = (mix_ref[...].astype(F32).T * 0.5).astype(BF)
    owb_ref[...] = jnp.broadcast_to(ow_ref[...], (CELL, LAT)).T
    own_ref[...] = jnp.zeros_like(own_ref)

    def prepare(t):
        swap = cb_ref[t] < ca_ref[t]
        slots = cell_slots(tf_ref[t])
        proj_a = dot(fa_ref[t], wa_ref[...], ((1,), (0,))).astype(BF).astype(F32)
        proj_b = dot(fb_ref[t], wb_ref[...], ((1,), (0,))).astype(BF).astype(F32)
        pr = jnp.where(swap, proj_b, proj_a) * 0.5
        pc = jnp.where(swap, proj_a, proj_b) * 0.5
        projc[t] = pc.T
        groups = pr.reshape(CELL // SUB, SUB, LAT)
        lead[t] = jnp.concatenate([groups, jnp.zeros_like(groups)], axis=1).astype(BF)
        xa = pos_ref[:, slots].astype(F32)
        xb = xb_ref[t]
        xr = jnp.where(swap, xb, xa)
        xc = jnp.where(swap, xa, xb)
        r2 = jnp.zeros((CELL, CELL), F32)
        for k in range(3):
            d = jnp.broadcast_to(xr[k : k + 1], (CELL, CELL)).T - jnp.broadcast_to(xc[k : k + 1], (CELL, CELL))
            diff_ref[t, k] = d
            r2 = r2 + d * d
        r2_ref[t] = r2 * SPREAD

    def prepare_four(u, _):
        for i in range(4):
            prepare(4 * u + i)
        return 0

    lax.fori_loop(0, tiles // 4, prepare_four, 0)

    hot = lax.broadcasted_iota(jnp.int32, (16, SUB * CELL), 0)
    hot = hot == lax.broadcasted_iota(jnp.int32, (16, SUB * CELL), 1) // CELL
    hot = hot.astype(F32).astype(BF)
    centers = lax.broadcasted_iota(jnp.int32, (NB, CELL), 0).astype(F32) * (STEP * SPREAD)
    n_sub = ROWS // SUB
    per_sub = SUB // PIECE

    def subs_of(t):
        return (jnp.minimum(ca_ref[t], cb_ref[t]) + SUB - 1) // SUB

    def following(place):
        places = []
        for _ in range(n_sub):
            t, c = place
            last = c + 1 >= subs_of(jnp.minimum(t, tiles - 1))
            place = jnp.where(last, jnp.minimum(t + 1, tiles), t), jnp.where(last, 0, c + 1)
            places.append(place)
        return tuple(places)

    def step(it, carry):
        at1, at2, at3, at4 = carry
        rows = lambda c: pl.ds(pl.multiple_of(c * SUB, SUB), SUB)
        slope_at = lax.rem(it, 2)
        z_at = lax.rem(it, 3)
        owb = jnp.concatenate([owb_ref[...]] * PIECE, axis=1)
        for p in range(ROWS // PIECE):
            cs = slice(p * PW, (p + 1) * PW)
            q = p % per_sub
            if q == 0:
                (t1, c1), (t2, _), (t3, c3), (t4, c4) = (at[p // per_sub] for at in carry)
                in1 = jnp.minimum(t1, tiles - 1)
                r2 = r2_ref[in1, rows(c1), :]
                lhs = jnp.concatenate([wr_ref[...] * jnp.asarray(0.5, BF), lead[in1, c1]], axis=0)
                pc = jnp.concatenate([projc[jnp.minimum(t2, tiles - 1)]] * PIECE, axis=1)
                cores = []
                readouts = []
            ds = (y_s[:, cs] * slope_s[slope_at, :, cs]).astype(BF)
            z = z_s[z_at, :, cs]
            h2 = h2_s[:, cs]
            tt = jnp.tanh(h2)
            v = owb * (1 + tt)
            act = h2 * v
            ro = jnp.sum(act, axis=0, keepdims=True)
            back = (v + act * (1 - tt)).astype(BF)
            h = h_s[:, cs] + pc
            tt = jnp.tanh(h)
            v = 1 + tt
            act = h * v
            slope_s[slope_at, :, cs] = v + act * (1 - tt)
            latent = act.astype(BF)
            gs = []
            zs = []
            for i in range(q * PIECE, (q + 1) * PIECE):
                o = jnp.broadcast_to(r2[i : i + 1], (NB, CELL)) - centers
                g = jnp.exp2(-(o * o))
                gs.append(g.astype(BF))
                zs.append(g * o)
            z_s[z_at, :, cs] = jnp.concatenate(zs, axis=1)
            rhs = jnp.concatenate([jnp.concatenate(gs, axis=1), hot[:, q * PW : (q + 1) * PW]], axis=0)
            y_s[:, cs] = dot(mix_ref[...], back, ((1,), (0,)))
            h_s[:, cs] = dot(lhs, rhs, ((0,), (0,)))
            z = dot(wr_ref[...], ds, ((1,), (0,))) * z
            h2_s[:, cs] = dot(mixt_ref[...], latent, ((1,), (0,)))
            for i in range(PIECE):
                cores.append(jnp.sum(z[:, i * CELL : (i + 1) * CELL], axis=0, keepdims=True))
                readouts.append(ro[:, i * CELL : (i + 1) * CELL])
            if q == per_sub - 1:
                d_ref[0, t4, rows(c4), :] = jnp.concatenate(cores, axis=0)
                d_ref[1, t3, rows(c3), :] = jnp.concatenate(readouts, axis=0)
        return following(at1[-1]), at1, at2, at3

    total = jnp.int32(0)
    for t in range(tiles):
        total = total + subs_of(t)
    zero = jnp.int32(0)
    start = (zero, zero)
    start = ((start,) + following(start))[:n_sub]
    idle = ((jnp.int32(tiles), zero),) * n_sub
    lax.fori_loop(0, (total + n_sub - 1) // n_sub + 3, step, (start, idle, idle, idle))

    def finish(t):
        ca, cb = ca_ref[t], cb_ref[t]
        swap = cb < ca
        row = lax.broadcasted_iota(jnp.int32, (CELL, CELL), 0)
        col = lax.broadcasted_iota(jnp.int32, (CELL, CELL), 1)
        live = (row < jnp.minimum(ca, cb)) & (col < jnp.maximum(ca, cb))
        env = 1 - r2_ref[t] * (0.125 / SPREAD)
        dd = env * env * (d_ref[0, t] * (-4.0 / (SPREAD * 4 * CELL))) + env * (d_ref[1, t] * (-0.25 / CELL))
        dd = jnp.where(live, 2 * dd, 0.0)
        gr = []
        gc = []
        for k in range(3):
            pull = diff_ref[t, k] * dd
            gr.append(jnp.sum(pull.T, axis=0, keepdims=True))
            gc.append(-jnp.sum(pull, axis=0, keepdims=True))
        gr = jnp.concatenate(gr, axis=0)
        gc = jnp.concatenate(gc, axis=0)
        return jnp.where(swap, gc, gr), jnp.where(swap, gr, gc)

    def put(t, ga, gb):
        own_ref[:, cell_slots(tf_ref[t])] -= ga
        gb_ref[t] = gb

        @pl.when(ts_ref[t] // CELLS == 0)
        def _():
            own_ref[:, cell_slots(lax.rem(ts_ref[t], CELLS))] -= gb

    def finish_four(u, _):
        found = [finish(4 * u + i) for i in range(4)]
        for i in range(4):
            put(4 * u + i, *found[i])
        return 0

    lax.fori_loop(0, tiles // 4, finish_four, 0)


def return_kernel(
    n_tiles, ask_any, own_any, second_ref, out_ref, ask_ref, own_ref, back_ref, load_sem, send_sem, recv_sem
):
    barrier = pltpu.get_barrier_semaphore()
    for g, d in WAYS:
        pl.semaphore_signal(barrier, inc=1, device_id=other(g, d), device_id_type=MESH)
    loads = [
        pltpu.make_async_copy(ask_any, ask_ref, load_sem.at[0]),
        pltpu.make_async_copy(own_any, own_ref, load_sem.at[1]),
    ]
    for load in loads:
        load.start()
    pl.semaphore_wait(barrier, len(WAYS))
    copies = []
    for w, (g, d) in enumerate(WAYS):
        copy = pltpu.make_async_remote_copy(
            src_ref=second_ref, dst_ref=back_ref.at[w], send_sem=send_sem.at[w], recv_sem=recv_sem.at[w],
            device_id=other(-g, -d), device_id_type=MESH,
        )
        copy.start()
        copies.append(copy)
    for copy in loads + copies:
        copy.wait()

    asked = [[ask_ref[w, t : t + 1, :] - (w + 1) * CELLS for t in range(n_tiles)] for w in range(len(WAYS))]

    def four(u, _):
        for i in range(4):
            c = 4 * u + i
            sums = []
            for w in range(len(WAYS)):
                hits = [jnp.where(asked[w][t] == c, back_ref[w, t], 0.0) for t in range(n_tiles)]
                while len(hits) > 1:
                    hits = [x + y for x, y in zip(hits[::2], hits[1::2], strict=True)]
                sums += hits
            slots = cell_slots(c)
            out_ref[:, slots] = own_ref[:, slots] - (sums[0] + sums[1] + sums[2])
        return 0

    lax.fori_loop(0, CELLS // 4, four, 0)


def on_device(
    positions, features, tile_first, tile_second, count_first, count_second, w_first, w_second, radial_weight,
    mix_weight, out_weight,
):
    tiles = tile_first.shape[0]
    smem = pl.BlockSpec(memory_space=pltpu.SMEM)
    vmem = pl.BlockSpec(memory_space=pltpu.VMEM)

    anywhere = pl.BlockSpec(memory_space=pl.ANY)
    dma = pltpu.SemaphoreType.DMA
    n = len(WAYS)
    cells = (tiles, CELL, LAT)
    ask, first, second, got_pos = pl.pallas_call(
        functools.partial(fetch_kernel, tiles),
        out_shape=[
            jax.ShapeDtypeStruct((n, tiles, CELL), jnp.int32),
            jax.ShapeDtypeStruct(cells, BF),
            jax.ShapeDtypeStruct(cells, BF),
            jax.ShapeDtypeStruct((n, *positions.shape), BF),
        ],
        in_specs=[smem, smem, anywhere, anywhere],
        out_specs=[vmem, vmem, vmem, anywhere],
        scratch_shapes=[
            pltpu.VMEM((CELLS, CELL, LAT), BF),
            dma(()),
            pltpu.VMEM((tiles, CELL), jnp.int32),
            pltpu.SMEM((n, tiles, CELL), jnp.int32),
        ]
        + [pltpu.VMEM(cells, BF)] * 6
        + [dma((n,))] * 3
        + [dma((GROUPS,))] * 4
        + [dma(())] * 2
        + [dma((n,))] * 2,
        compiler_params=pltpu.CompilerParams(collective_id=0, has_side_effects=True),
        name="fetch",
    )(tile_first, tile_second, positions, features.reshape(-1, CELL, LAT))
    W = ROWS * CELL
    own, partial = pl.pallas_call(
        tile_kernel,
        out_shape=[jax.ShapeDtypeStruct(positions.shape, F32), jax.ShapeDtypeStruct((tiles, 3, CELL), F32)],
        in_specs=[smem] * 4 + [vmem] * 9,
        out_specs=[vmem] * 2,
        scratch_shapes=[
            pltpu.VMEM((tiles, 3, CELL), F32),
            pltpu.VMEM((LAT, LAT), BF),
            pltpu.VMEM((LAT, CELL), F32),
            pltpu.VMEM((tiles, CELL // SUB, 16, LAT), BF),
            pltpu.VMEM((tiles, LAT, CELL), F32),
            pltpu.VMEM((2, tiles + 1, CELL, CELL), F32),
            pltpu.VMEM((tiles, CELL, CELL), F32),
            pltpu.VMEM((tiles, 3, CELL, CELL), F32),
            pltpu.VMEM((LAT, W), F32),
            pltpu.VMEM((LAT, W), F32),
            pltpu.VMEM((LAT, W), F32),
            pltpu.VMEM((2, LAT, W), F32),
            pltpu.VMEM((3, NB, W), F32),
        ],
        compiler_params=pltpu.CompilerParams(vmem_limit_bytes=60 << 20),
        name="tiles",
    )(
        tile_first, tile_second, count_first, count_second, positions, got_pos, first, second, w_first, w_second,
        radial_weight, mix_weight, out_weight.reshape(1, LAT),
    )
    return pl.pallas_call(
        functools.partial(return_kernel, tiles),
        out_shape=jax.ShapeDtypeStruct(positions.shape, F32),
        in_specs=[anywhere] * 3,
        out_specs=vmem,
        scratch_shapes=[
            pltpu.VMEM((n, tiles, CELL), jnp.int32),
            pltpu.VMEM(positions.shape, F32),
            pltpu.VMEM((n, tiles, 3, CELL), F32),
            dma((2,)),
            dma((n,)),
            dma((n,)),
        ],
        compiler_params=pltpu.CompilerParams(collective_id=1, has_side_effects=True),
        name="return",
    )(ask, own, partial)


def solution(mesh):
    each = P(("grp", "dev"))
    in_specs = (P(None, ("grp", "dev")), P(("grp", "dev"), None), each, each, each, each, P(), P(), P(), P(), P())
    return jax.shard_map(
        on_device, mesh=mesh, in_specs=in_specs, out_specs=P(None, ("grp", "dev")), check_vma=False
    )
```

```python
import functools

import jax
import jax.numpy as jnp
from jax import lax
from jax.experimental import pallas as pl
from jax.experimental.pallas import tpu as pltpu
from jax.sharding import PartitionSpec as P

CELL = 128
CELLS = 32
LAT = 128
NB = 16
ROWS = 24
SUB = 8
PIECE = 2
GROUPS = 4
WAYS = ((0, 1), (1, 0), (1, 1))
MESH = pl.DeviceIdType.MESH
SPREAD = 2.8853900817779268**0.5
STEP = 6.75 / NB
F32 = jnp.float32
BF = jnp.bfloat16


def dot(a, b, dims):
    return lax.dot_general(a, b, (dims, ((), ())), preferred_element_type=F32)


def cell_slots(cell):
    return pl.ds(pl.multiple_of(cell * CELL, CELL), CELL)


def other(by_grp, by_dev):
    g = lax.axis_index("grp") + by_grp
    d = lax.axis_index("dev") + by_dev
    n_grp = lax.axis_size("grp")
    n_dev = lax.axis_size("dev")
    return lax.rem(g + n_grp, n_grp), lax.rem(d + n_dev, n_dev)


def remote(src, dst, send, recv, to):
    copy = pltpu.make_async_remote_copy(
        src_ref=src, dst_ref=dst, send_sem=send, recv_sem=recv, device_id=to, device_id_type=MESH
    )
    copy.start()
    return copy


def fetch_kernel(
    n_tiles, tf_ref, ts_ref, pos_any, feat_any, ask_ref, fa_ref, fb_ref, gotpos_ref,
    feat_ref, feat_sem, mine, numbers, corner_out, corner_in, side_out, side_in, up_out, up_in,
    ask_send, ask_recv, local_sem, corner_send, corner_recv, up_send, up_recv, side_send, side_recv, pos_send, pos_recv,
):
    features = pltpu.make_async_copy(feat_any, feat_ref, feat_sem)
    features.start()
    barrier = pltpu.get_barrier_semaphore()
    for g, d in WAYS:
        pl.semaphore_signal(barrier, inc=1, device_id=other(g, d), device_id_type=MESH)
        pl.semaphore_signal(barrier, inc=1, device_id=other(-g, -d), device_id_type=MESH)
    for t in range(n_tiles):
        mine[t : t + 1, :] = jnp.full((1, CELL), ts_ref[t], jnp.int32)
    pl.semaphore_wait(barrier, 2 * len(WAYS))

    asks = {}
    for w in (2, 0, 1):
        g, d = WAYS[w]
        asks[w] = remote(mine, ask_ref.at[w], ask_send.at[w], ask_recv.at[w], other(-g, -d))
    sent = [
        remote(pos_any, gotpos_ref.at[w], pos_send.at[w], pos_recv.at[w], other(g, d)) for w, (g, d) in enumerate(WAYS)
    ]
    features.wait()

    def hear(w):
        asks[w].wait_recv()
        local = pltpu.make_async_copy(ask_ref.at[w], numbers.at[w], local_sem.at[w])
        local.start()
        local.wait()

    def pick(w, t):
        return feat_ref[lax.rem(numbers[w, t, 0], CELLS)]

    hear(2)
    corners = []
    for j in range(GROUPS):
        part = range(j * n_tiles // GROUPS, (j + 1) * n_tiles // GROUPS)
        for t in part:
            corner_out[t] = pick(2, t)
        at = pl.ds(part.start, len(part))
        corners.append(
            remote(corner_out.at[at], corner_in.at[at], corner_send.at[j], corner_recv.at[j], other(0, 1))
        )
    hear(0)
    for t in range(n_tiles):
        side_out[t] = pick(0, t)
    sides = remote(side_out, side_in, side_send, side_recv, other(0, 1))
    hear(1)
    for t in range(n_tiles):
        up_out[t] = pick(1, t)
    ups = []
    for j in range(GROUPS):
        part = range(j * n_tiles // GROUPS, (j + 1) * n_tiles // GROUPS)
        corners[j].wait_recv()
        for t in part:
            near = ask_ref[1, t : t + 1, :] < 3 * CELLS
            up_out[t] = jnp.where(near, up_out[t].astype(F32), corner_in[t].astype(F32)).astype(BF)
        at = pl.ds(part.start, len(part))
        ups.append(remote(up_out.at[at], up_in.at[at], up_send.at[j], up_recv.at[j], other(1, 0)))
    for t in range(n_tiles):
        fa_ref[t] = feat_ref[tf_ref[t]]
        fb_ref[t] = feat_ref[lax.rem(ts_ref[t], CELLS)]
    sides.wait_recv()
    for t in range(n_tiles):
        own = mine[t : t + 1, :] < CELLS
        fb_ref[t] = jnp.where(own, fb_ref[t].astype(F32), side_in[t].astype(F32)).astype(BF)
    for j in range(GROUPS):
        ups[j].wait_recv()
        for t in range(j * n_tiles // GROUPS, (j + 1) * n_tiles // GROUPS):
            near = mine[t : t + 1, :] < 2 * CELLS
            fb_ref[t] = jnp.where(near, fb_ref[t].astype(F32), up_in[t].astype(F32)).astype(BF)
    for copy in sent:
        copy.wait()
    for copy in list(asks.values()) + corners + [sides] + ups:
        copy.wait_send()


def tile_kernel(
    tf_ref, ts_ref, ca_ref, cb_ref, pos_ref, gotpos_ref, fa_ref, fb_ref, wa_ref, wb_ref, wr_ref, mix_ref, ow_ref,
    own_ref, gb_ref,
    xb_ref, mixt_ref, owb_ref, lead, projc, d_ref, r2_ref, diff_ref, h_s, h2_s, y_s, slope_s, z_s,
):
    W = ROWS * CELL
    PW = PIECE * CELL
    tiles = gb_ref.shape[0]

    for t in range(tiles):
        slots = cell_slots(lax.rem(ts_ref[t], CELLS))
        source = ts_ref[t] // CELLS
        came = gotpos_ref[jnp.maximum(source - 1, 0), :, slots].astype(F32)
        xb_ref[t] = jnp.where(source == 0, pos_ref[:, slots].astype(F32), came)
    mixt_ref[...] = (mix_ref[...].astype(F32).T * 0.5).astype(BF)
    owb_ref[...] = jnp.broadcast_to(ow_ref[...], (CELL, LAT)).T
    own_ref[...] = jnp.zeros_like(own_ref)

    def prepare(t):
        swap = cb_ref[t] < ca_ref[t]
        slots = cell_slots(tf_ref[t])
        proj_a = dot(fa_ref[t], wa_ref[...], ((1,), (0,))).astype(BF).astype(F32)
        proj_b = dot(fb_ref[t], wb_ref[...], ((1,), (0,))).astype(BF).astype(F32)
        pr = jnp.where(swap, proj_b, proj_a) * 0.5
        pc = jnp.where(swap, proj_a, proj_b) * 0.5
        projc[t] = pc.T
        groups = pr.reshape(CELL // SUB, SUB, LAT)
        lead[t] = jnp.concatenate([groups, jnp.zeros_like(groups)], axis=1).astype(BF)
        xa = pos_ref[:, slots].astype(F32)
        xb = xb_ref[t]
        xr = jnp.where(swap, xb, xa)
        xc = jnp.where(swap, xa, xb)
        r2 = jnp.zeros((CELL, CELL), F32)
        for k in range(3):
            d = jnp.broadcast_to(xr[k : k + 1], (CELL, CELL)).T - jnp.broadcast_to(xc[k : k + 1], (CELL, CELL))
            diff_ref[t, k] = d
            r2 = r2 + d * d
        r2_ref[t] = r2 * SPREAD

    def prepare_four(u, _):
        for i in range(4):
            prepare(4 * u + i)
        return 0

    lax.fori_loop(0, tiles // 4, prepare_four, 0)

    hot = lax.broadcasted_iota(jnp.int32, (16, SUB * CELL), 0)
    hot = hot == lax.broadcasted_iota(jnp.int32, (16, SUB * CELL), 1) // CELL
    hot = hot.astype(F32).astype(BF)
    centers = lax.broadcasted_iota(jnp.int32, (NB, CELL), 0).astype(F32) * (STEP * SPREAD)
    n_sub = ROWS // SUB
    per_sub = SUB // PIECE

    def subs_of(t):
        return (jnp.minimum(ca_ref[t], cb_ref[t]) + SUB - 1) // SUB

    def following(place):
        places = []
        for _ in range(n_sub):
            t, c = place
            last = c + 1 >= subs_of(jnp.minimum(t, tiles - 1))
            place = jnp.where(last, jnp.minimum(t + 1, tiles), t), jnp.where(last, 0, c + 1)
            places.append(place)
        return tuple(places)

    def step(it, carry):
        before, now = carry
        places = before + now
        rows = lambda c: pl.ds(pl.multiple_of(c * SUB, SUB), SUB)
        owb = jnp.concatenate([owb_ref[...]] * PIECE, axis=1)
        for p in range(ROWS // PIECE):
            cs, cs2, cs3, _ = (
                slice(k * PW, (k + 1) * PW) for k in ((p - lag * per_sub) % (n_sub * per_sub) for lag in range(4))
            )
            q = p % per_sub
            if q == 0:
                at = n_sub + p // per_sub
                (t1, c1), (t2, _), (t3, c3), (t4, c4) = (places[at - lag] for lag in range(4))
                in1 = jnp.minimum(t1, tiles - 1)
                r2 = r2_ref[in1, rows(c1), :]
                lhs = jnp.concatenate([wr_ref[...] * jnp.asarray(0.5, BF), lead[in1, c1]], axis=0)
                pc = jnp.concatenate([projc[jnp.minimum(t2, tiles - 1)]] * PIECE, axis=1)
                cores = []
                readouts = []
            ds = (y_s[:, cs] * slope_s[:, cs]).astype(BF)
            z = z_s[:, cs]
            h2 = h2_s[:, cs3]
            tt = jnp.tanh(h2)
            v = owb * (1 + tt)
            act = h2 * v
            ro = jnp.sum(act, axis=0, keepdims=True)
            back = (v + act * (1 - tt)).astype(BF)
            h = h_s[:, cs2] + pc
            tt = jnp.tanh(h)
            v = 1 + tt
            act = h * v
            slope_s[:, cs2] = v + act * (1 - tt)
            latent = act.astype(BF)
            gs = []
            zs = []
            for i in range(q * PIECE, (q + 1) * PIECE):
                o = jnp.broadcast_to(r2[i : i + 1], (NB, CELL)) - centers
                g = jnp.exp2(-(o * o))
                gs.append(g.astype(BF))
                zs.append(g * o)
            z_s[:, cs] = jnp.concatenate(zs, axis=1)
            rhs = jnp.concatenate([jnp.concatenate(gs, axis=1), hot[:, q * PW : (q + 1) * PW]], axis=0)
            y_s[:, cs3] = dot(mix_ref[...], back, ((1,), (0,)))
            h_s[:, cs] = dot(lhs, rhs, ((0,), (0,)))
            z = dot(wr_ref[...], ds, ((1,), (0,))) * z
            h2_s[:, cs2] = dot(mixt_ref[...], latent, ((1,), (0,)))
            for i in range(PIECE):
                cores.append(jnp.sum(z[:, i * CELL : (i + 1) * CELL], axis=0, keepdims=True))
                readouts.append(ro[:, i * CELL : (i + 1) * CELL])
            if q == per_sub - 1:
                d_ref[0, t4, rows(c4), :] = jnp.concatenate(cores, axis=0)
                d_ref[1, t3, rows(c3), :] = jnp.concatenate(readouts, axis=0)
        return now, following(now[-1])

    total = jnp.int32(0)
    for t in range(tiles):
        total = total + subs_of(t)
    zero = jnp.int32(0)
    start = (zero, zero)
    start = ((start,) + following(start))[:n_sub]
    idle = ((jnp.int32(tiles), zero),) * n_sub
    lax.fori_loop(0, (total + n_sub + 2) // n_sub, step, (idle, start))

    def finish(t):
        ca, cb = ca_ref[t], cb_ref[t]
        swap = cb < ca
        row = lax.broadcasted_iota(jnp.int32, (CELL, CELL), 0)
        col = lax.broadcasted_iota(jnp.int32, (CELL, CELL), 1)
        live = (row < jnp.minimum(ca, cb)) & (col < jnp.maximum(ca, cb))
        env = 1 - r2_ref[t] * (0.125 / SPREAD)
        dd = env * env * (d_ref[0, t] * (-4.0 / (SPREAD * 4 * CELL))) + env * (d_ref[1, t] * (-0.25 / CELL))
        dd = jnp.where(live, 2 * dd, 0.0)
        gr = []
        gc = []
        for k in range(3):
            pull = diff_ref[t, k] * dd
            gr.append(jnp.sum(pull.T, axis=0, keepdims=True))
            gc.append(-jnp.sum(pull, axis=0, keepdims=True))
        gr = jnp.concatenate(gr, axis=0)
        gc = jnp.concatenate(gc, axis=0)
        return jnp.where(swap, gc, gr), jnp.where(swap, gr, gc)

    def put(t, ga, gb):
        own_ref[:, cell_slots(tf_ref[t])] -= ga
        gb_ref[t] = gb

        @pl.when(ts_ref[t] // CELLS == 0)
        def _():
            own_ref[:, cell_slots(lax.rem(ts_ref[t], CELLS))] -= gb

    def finish_four(u, _):
        found = [finish(4 * u + i) for i in range(4)]
        for i in range(4):
            put(4 * u + i, *found[i])
        return 0

    lax.fori_loop(0, tiles // 4, finish_four, 0)


def return_kernel(
    n_tiles, ask_any, own_any, second_ref, out_ref, ask_ref, own_ref, back_ref, load_sem, send_sem, recv_sem
):
    barrier = pltpu.get_barrier_semaphore()
    for g, d in WAYS:
        pl.semaphore_signal(barrier, inc=1, device_id=other(g, d), device_id_type=MESH)
    loads = [
        pltpu.make_async_copy(ask_any, ask_ref, load_sem.at[0]),
        pltpu.make_async_copy(own_any, own_ref, load_sem.at[1]),
    ]
    for load in loads:
        load.start()
    pl.semaphore_wait(barrier, len(WAYS))
    copies = []
    for w, (g, d) in enumerate(WAYS):
        copy = pltpu.make_async_remote_copy(
            src_ref=second_ref, dst_ref=back_ref.at[w], send_sem=send_sem.at[w], recv_sem=recv_sem.at[w],
            device_id=other(-g, -d), device_id_type=MESH,
        )
        copy.start()
        copies.append(copy)
    for copy in loads + copies:
        copy.wait()

    asked = [[ask_ref[w, t : t + 1, :] - (w + 1) * CELLS for t in range(n_tiles)] for w in range(len(WAYS))]

    def four(u, _):
        for i in range(4):
            c = 4 * u + i
            sums = []
            for w in range(len(WAYS)):
                hits = [jnp.where(asked[w][t] == c, back_ref[w, t], 0.0) for t in range(n_tiles)]
                while len(hits) > 1:
                    hits = [x + y for x, y in zip(hits[::2], hits[1::2], strict=True)]
                sums += hits
            slots = cell_slots(c)
            out_ref[:, slots] = own_ref[:, slots] - (sums[0] + sums[1] + sums[2])
        return 0

    lax.fori_loop(0, CELLS // 4, four, 0)


def on_device(
    positions, features, tile_first, tile_second, count_first, count_second, w_first, w_second, radial_weight,
    mix_weight, out_weight,
):
    tiles = tile_first.shape[0]
    smem = pl.BlockSpec(memory_space=pltpu.SMEM)
    vmem = pl.BlockSpec(memory_space=pltpu.VMEM)

    anywhere = pl.BlockSpec(memory_space=pl.ANY)
    dma = pltpu.SemaphoreType.DMA
    n = len(WAYS)
    cells = (tiles, CELL, LAT)
    ask, first, second, got_pos = pl.pallas_call(
        functools.partial(fetch_kernel, tiles),
        out_shape=[
            jax.ShapeDtypeStruct((n, tiles, CELL), jnp.int32),
            jax.ShapeDtypeStruct(cells, BF),
            jax.ShapeDtypeStruct(cells, BF),
            jax.ShapeDtypeStruct((n, *positions.shape), BF),
        ],
        in_specs=[smem, smem, anywhere, anywhere],
        out_specs=[vmem, vmem, vmem, anywhere],
        scratch_shapes=[
            pltpu.VMEM((CELLS, CELL, LAT), BF),
            dma(()),
            pltpu.VMEM((tiles, CELL), jnp.int32),
            pltpu.SMEM((n, tiles, CELL), jnp.int32),
        ]
        + [pltpu.VMEM(cells, BF)] * 6
        + [dma((n,))] * 3
        + [dma((GROUPS,))] * 4
        + [dma(())] * 2
        + [dma((n,))] * 2,
        compiler_params=pltpu.CompilerParams(collective_id=0, has_side_effects=True),
        name="fetch",
    )(tile_first, tile_second, positions, features.reshape(-1, CELL, LAT))
    W = ROWS * CELL
    own, partial = pl.pallas_call(
        tile_kernel,
        out_shape=[jax.ShapeDtypeStruct(positions.shape, F32), jax.ShapeDtypeStruct((tiles, 3, CELL), F32)],
        in_specs=[smem] * 4 + [vmem] * 9,
        out_specs=[vmem] * 2,
        scratch_shapes=[
            pltpu.VMEM((tiles, 3, CELL), F32),
            pltpu.VMEM((LAT, LAT), BF),
            pltpu.VMEM((LAT, CELL), F32),
            pltpu.VMEM((tiles, CELL // SUB, 16, LAT), BF),
            pltpu.VMEM((tiles, LAT, CELL), F32),
            pltpu.VMEM((2, tiles + 1, CELL, CELL), F32),
            pltpu.VMEM((tiles, CELL, CELL), F32),
            pltpu.VMEM((tiles, 3, CELL, CELL), F32),
            pltpu.VMEM((LAT, W), F32),
            pltpu.VMEM((LAT, W), F32),
            pltpu.VMEM((LAT, W), F32),
            pltpu.VMEM((LAT, W), F32),
            pltpu.VMEM((NB, W), F32),
        ],
        compiler_params=pltpu.CompilerParams(vmem_limit_bytes=60 << 20),
        name="tiles",
    )(
        tile_first, tile_second, count_first, count_second, positions, got_pos, first, second, w_first, w_second,
        radial_weight, mix_weight, out_weight.reshape(1, LAT),
    )
    return pl.pallas_call(
        functools.partial(return_kernel, tiles),
        out_shape=jax.ShapeDtypeStruct(positions.shape, F32),
        in_specs=[anywhere] * 3,
        out_specs=vmem,
        scratch_shapes=[
            pltpu.VMEM((n, tiles, CELL), jnp.int32),
            pltpu.VMEM(positions.shape, F32),
            pltpu.VMEM((n, tiles, 3, CELL), F32),
            dma((2,)),
            dma((n,)),
            dma((n,)),
        ],
        compiler_params=pltpu.CompilerParams(collective_id=1, has_side_effects=True),
        name="return",
    )(ask, own, partial)


def solution(mesh):
    each = P(("grp", "dev"))
    in_specs = (P(None, ("grp", "dev")), P(("grp", "dev"), None), each, each, each, each, P(), P(), P(), P(), P())
    return jax.shard_map(
        on_device, mesh=mesh, in_specs=in_specs, out_specs=P(None, ("grp", "dev")), check_vma=False
    )
```

```python
import functools

import jax
import jax.numpy as jnp
from jax import lax
from jax.experimental import pallas as pl
from jax.experimental.pallas import tpu as pltpu
from jax.sharding import PartitionSpec as P

CELL = 128
CELLS = 32
LAT = 128
NB = 16
ROWS = 32
SUB = 8
PIECE = 2
GROUPS = 4
WAYS = ((0, 1), (1, 0), (1, 1))
MESH = pl.DeviceIdType.MESH
SPREAD = 2.8853900817779268**0.5
STEP = 6.75 / NB
F32 = jnp.float32
BF = jnp.bfloat16


def dot(a, b, dims):
    return lax.dot_general(a, b, (dims, ((), ())), preferred_element_type=F32)


def cell_slots(cell):
    return pl.ds(pl.multiple_of(cell * CELL, CELL), CELL)


def other(by_grp, by_dev):
    g = lax.axis_index("grp") + by_grp
    d = lax.axis_index("dev") + by_dev
    n_grp = lax.axis_size("grp")
    n_dev = lax.axis_size("dev")
    return lax.rem(g + n_grp, n_grp), lax.rem(d + n_dev, n_dev)


def remote(src, dst, send, recv, to):
    copy = pltpu.make_async_remote_copy(
        src_ref=src, dst_ref=dst, send_sem=send, recv_sem=recv, device_id=to, device_id_type=MESH
    )
    copy.start()
    return copy


def fetch_kernel(
    n_tiles, tf_ref, ts_ref, pos_any, feat_any, ask_ref, fa_ref, fb_ref, gotpos_ref,
    feat_ref, feat_sem, mine, numbers, corner_out, corner_in, side_out, side_in, up_out, up_in,
    ask_send, ask_recv, local_sem, corner_send, corner_recv, up_send, up_recv, side_send, side_recv, pos_send, pos_recv,
):
    features = pltpu.make_async_copy(feat_any, feat_ref, feat_sem)
    features.start()
    barrier = pltpu.get_barrier_semaphore()
    for g, d in WAYS:
        pl.semaphore_signal(barrier, inc=1, device_id=other(g, d), device_id_type=MESH)
        pl.semaphore_signal(barrier, inc=1, device_id=other(-g, -d), device_id_type=MESH)
    for t in range(n_tiles):
        mine[t : t + 1, :] = jnp.full((1, CELL), ts_ref[t], jnp.int32)
    pl.semaphore_wait(barrier, 2 * len(WAYS))

    asks = {}
    for w in (2, 0, 1):
        g, d = WAYS[w]
        asks[w] = remote(mine, ask_ref.at[w], ask_send.at[w], ask_recv.at[w], other(-g, -d))
    sent = [
        remote(pos_any, gotpos_ref.at[w], pos_send.at[w], pos_recv.at[w], other(g, d)) for w, (g, d) in enumerate(WAYS)
    ]
    features.wait()

    def hear(w):
        asks[w].wait_recv()
        local = pltpu.make_async_copy(ask_ref.at[w], numbers.at[w], local_sem.at[w])
        local.start()
        local.wait()

    def pick(w, t):
        return feat_ref[lax.rem(numbers[w, t, 0], CELLS)]

    hear(2)
    corners = []
    for j in range(GROUPS):
        part = range(j * n_tiles // GROUPS, (j + 1) * n_tiles // GROUPS)
        for t in part:
            corner_out[t] = pick(2, t)
        at = pl.ds(part.start, len(part))
        corners.append(
            remote(corner_out.at[at], corner_in.at[at], corner_send.at[j], corner_recv.at[j], other(0, 1))
        )
    hear(0)
    for t in range(n_tiles):
        side_out[t] = pick(0, t)
    sides = remote(side_out, side_in, side_send, side_recv, other(0, 1))
    hear(1)
    for t in range(n_tiles):
        up_out[t] = pick(1, t)
    ups = []
    for j in range(GROUPS):
        part = range(j * n_tiles // GROUPS, (j + 1) * n_tiles // GROUPS)
        corners[j].wait_recv()
        for t in part:
            near = ask_ref[1, t : t + 1, :] < 3 * CELLS
            up_out[t] = jnp.where(near, up_out[t].astype(F32), corner_in[t].astype(F32)).astype(BF)
        at = pl.ds(part.start, len(part))
        ups.append(remote(up_out.at[at], up_in.at[at], up_send.at[j], up_recv.at[j], other(1, 0)))
    for t in range(n_tiles):
        fa_ref[t] = feat_ref[tf_ref[t]]
        fb_ref[t] = feat_ref[lax.rem(ts_ref[t], CELLS)]
    sides.wait_recv()
    for t in range(n_tiles):
        own = mine[t : t + 1, :] < CELLS
        fb_ref[t] = jnp.where(own, fb_ref[t].astype(F32), side_in[t].astype(F32)).astype(BF)
    for j in range(GROUPS):
        ups[j].wait_recv()
        for t in range(j * n_tiles // GROUPS, (j + 1) * n_tiles // GROUPS):
            near = mine[t : t + 1, :] < 2 * CELLS
            fb_ref[t] = jnp.where(near, fb_ref[t].astype(F32), up_in[t].astype(F32)).astype(BF)
    for copy in sent:
        copy.wait()
    for copy in list(asks.values()) + corners + [sides] + ups:
        copy.wait_send()


def tile_kernel(
    tf_ref, ts_ref, ca_ref, cb_ref, pos_ref, gotpos_ref, fa_ref, fb_ref, wa_ref, wb_ref, wr_ref, mix_ref, ow_ref,
    own_ref, gb_ref,
    xb_ref, mixt_ref, owb_ref, lead, projc, d_ref, r2_ref, diff_ref, h_s, h2_s, y_s, slope_s, z_s,
):
    W = ROWS * CELL
    PW = PIECE * CELL
    tiles = gb_ref.shape[0]

    for t in range(tiles):
        slots = cell_slots(lax.rem(ts_ref[t], CELLS))
        source = ts_ref[t] // CELLS
        came = gotpos_ref[jnp.maximum(source - 1, 0), :, slots].astype(F32)
        xb_ref[t] = jnp.where(source == 0, pos_ref[:, slots].astype(F32), came)
    mixt_ref[...] = (mix_ref[...].astype(F32).T * 0.5).astype(BF)
    owb_ref[...] = jnp.broadcast_to(ow_ref[...], (CELL, LAT)).T
    own_ref[...] = jnp.zeros_like(own_ref)

    def prepare(t):
        swap = cb_ref[t] < ca_ref[t]
        slots = cell_slots(tf_ref[t])
        proj_a = dot(fa_ref[t], wa_ref[...], ((1,), (0,))).astype(BF).astype(F32)
        proj_b = dot(fb_ref[t], wb_ref[...], ((1,), (0,))).astype(BF).astype(F32)
        pr = jnp.where(swap, proj_b, proj_a) * 0.5
        pc = jnp.where(swap, proj_a, proj_b) * 0.5
        projc[t] = pc.T
        groups = pr.reshape(CELL // SUB, SUB, LAT)
        lead[t] = jnp.concatenate([groups, jnp.zeros_like(groups)], axis=1).astype(BF)
        xa = pos_ref[:, slots].astype(F32)
        xb = xb_ref[t]
        xr = jnp.where(swap, xb, xa)
        xc = jnp.where(swap, xa, xb)
        r2 = jnp.zeros((CELL, CELL), F32)
        for k in range(3):
            d = jnp.broadcast_to(xr[k : k + 1], (CELL, CELL)).T - jnp.broadcast_to(xc[k : k + 1], (CELL, CELL))
            diff_ref[t, k] = d
            r2 = r2 + d * d
        r2_ref[t] = r2 * SPREAD

    def prepare_four(u, _):
        for i in range(4):
            prepare(4 * u + i)
        return 0

    lax.fori_loop(0, tiles // 4, prepare_four, 0)

    hot = lax.broadcasted_iota(jnp.int32, (16, SUB * CELL), 0)
    hot = hot == lax.broadcasted_iota(jnp.int32, (16, SUB * CELL), 1) // CELL
    hot = hot.astype(F32).astype(BF)
    centers = lax.broadcasted_iota(jnp.int32, (NB, CELL), 0).astype(F32) * (STEP * SPREAD)
    n_sub = ROWS // SUB
    per_sub = SUB // PIECE

    def subs_of(t):
        return (jnp.minimum(ca_ref[t], cb_ref[t]) + SUB - 1) // SUB

    def following(place):
        places = []
        for _ in range(n_sub):
            t, c = place
            last = c + 1 >= subs_of(jnp.minimum(t, tiles - 1))
            place = jnp.where(last, jnp.minimum(t + 1, tiles), t), jnp.where(last, 0, c + 1)
            places.append(place)
        return tuple(places)

    def step(it, carry):
        before, now = carry
        places = before + now
        rows = lambda c: pl.ds(pl.multiple_of(c * SUB, SUB), SUB)
        owb = jnp.concatenate([owb_ref[...]] * PIECE, axis=1)
        for p in range(ROWS // PIECE):
            cs, cs2, cs3, cs4 = (
                slice(k * PW, (k + 1) * PW) for k in ((p - lag * per_sub) % (n_sub * per_sub) for lag in range(4))
            )
            q = p % per_sub
            if q == 0:
                at = n_sub + p // per_sub
                (t1, c1), (t2, _), (t3, c3), (t4, c4) = (places[at - lag] for lag in range(4))
                in1 = jnp.minimum(t1, tiles - 1)
                r2 = r2_ref[in1, rows(c1), :]
                lhs = jnp.concatenate([wr_ref[...] * jnp.asarray(0.5, BF), lead[in1, c1]], axis=0)
                pc = jnp.concatenate([projc[jnp.minimum(t2, tiles - 1)]] * PIECE, axis=1)
                cores = []
                readouts = []
            ds = (y_s[:, cs4] * slope_s[:, cs4]).astype(BF)
            z = z_s[:, cs4]
            h2 = h2_s[:, cs3]
            tt = jnp.tanh(h2)
            v = owb * (1 + tt)
            act = h2 * v
            ro = jnp.sum(act, axis=0, keepdims=True)
            back = (v + act * (1 - tt)).astype(BF)
            h = h_s[:, cs2] + pc
            tt = jnp.tanh(h)
            v = 1 + tt
            act = h * v
            slope_s[:, cs2] = v + act * (1 - tt)
            latent = act.astype(BF)
            gs = []
            zs = []
            for i in range(q * PIECE, (q + 1) * PIECE):
                o = jnp.broadcast_to(r2[i : i + 1], (NB, CELL)) - centers
                g = jnp.exp2(-(o * o))
                gs.append(g.astype(BF))
                zs.append(g * o)
            z_s[:, cs] = jnp.concatenate(zs, axis=1)
            rhs = jnp.concatenate([jnp.concatenate(gs, axis=1), hot[:, q * PW : (q + 1) * PW]], axis=0)
            h2_s[:, cs2] = dot(mixt_ref[...], latent, ((1,), (0,)))
            z = dot(wr_ref[...], ds, ((1,), (0,))) * z
            h_s[:, cs] = dot(lhs, rhs, ((0,), (0,)))
            y_s[:, cs3] = dot(mix_ref[...], back, ((1,), (0,)))
            for i in range(PIECE):
                cores.append(jnp.sum(z[:, i * CELL : (i + 1) * CELL], axis=0, keepdims=True))
                readouts.append(ro[:, i * CELL : (i + 1) * CELL])
            if q == per_sub - 1:
                d_ref[0, t4, rows(c4), :] = jnp.concatenate(cores, axis=0)
                d_ref[1, t3, rows(c3), :] = jnp.concatenate(readouts, axis=0)
        return now, following(now[-1])

    total = jnp.int32(0)
    for t in range(tiles):
        total = total + subs_of(t)
    zero = jnp.int32(0)
    start = (zero, zero)
    start = ((start,) + following(start))[:n_sub]
    idle = ((jnp.int32(tiles), zero),) * n_sub
    lax.fori_loop(0, (total + n_sub + 2) // n_sub, step, (idle, start))

    def finish(t):
        ca, cb = ca_ref[t], cb_ref[t]
        swap = cb < ca
        row = lax.broadcasted_iota(jnp.int32, (CELL, CELL), 0)
        col = lax.broadcasted_iota(jnp.int32, (CELL, CELL), 1)
        live = (row < jnp.minimum(ca, cb)) & (col < jnp.maximum(ca, cb))
        env = 1 - r2_ref[t] * (0.125 / SPREAD)
        dd = env * env * (d_ref[0, t] * (-4.0 / (SPREAD * 4 * CELL))) + env * (d_ref[1, t] * (-0.25 / CELL))
        dd = jnp.where(live, 2 * dd, 0.0)
        gr = []
        gc = []
        for k in range(3):
            pull = diff_ref[t, k] * dd
            gr.append(jnp.sum(pull.T, axis=0, keepdims=True))
            gc.append(-jnp.sum(pull, axis=0, keepdims=True))
        gr = jnp.concatenate(gr, axis=0)
        gc = jnp.concatenate(gc, axis=0)
        return jnp.where(swap, gc, gr), jnp.where(swap, gr, gc)

    def put(t, ga, gb):
        own_ref[:, cell_slots(tf_ref[t])] -= ga
        gb_ref[t] = gb

        @pl.when(ts_ref[t] // CELLS == 0)
        def _():
            own_ref[:, cell_slots(lax.rem(ts_ref[t], CELLS))] -= gb

    def finish_four(u, _):
        found = [finish(4 * u + i) for i in range(4)]
        for i in range(4):
            put(4 * u + i, *found[i])
        return 0

    lax.fori_loop(0, tiles // 4, finish_four, 0)


def return_kernel(
    n_tiles, ask_any, own_any, second_ref, out_ref, ask_ref, own_ref, back_ref, load_sem, send_sem, recv_sem
):
    barrier = pltpu.get_barrier_semaphore()
    for g, d in WAYS:
        pl.semaphore_signal(barrier, inc=1, device_id=other(g, d), device_id_type=MESH)
    loads = [
        pltpu.make_async_copy(ask_any, ask_ref, load_sem.at[0]),
        pltpu.make_async_copy(own_any, own_ref, load_sem.at[1]),
    ]
    for load in loads:
        load.start()
    pl.semaphore_wait(barrier, len(WAYS))
    copies = []
    for w, (g, d) in enumerate(WAYS):
        copy = pltpu.make_async_remote_copy(
            src_ref=second_ref, dst_ref=back_ref.at[w], send_sem=send_sem.at[w], recv_sem=recv_sem.at[w],
            device_id=other(-g, -d), device_id_type=MESH,
        )
        copy.start()
        copies.append(copy)
    for copy in loads + copies:
        copy.wait()

    asked = [[ask_ref[w, t : t + 1, :] - (w + 1) * CELLS for t in range(n_tiles)] for w in range(len(WAYS))]

    def four(u, _):
        for i in range(4):
            c = 4 * u + i
            sums = []
            for w in range(len(WAYS)):
                hits = [jnp.where(asked[w][t] == c, back_ref[w, t], 0.0) for t in range(n_tiles)]
                while len(hits) > 1:
                    hits = [x + y for x, y in zip(hits[::2], hits[1::2], strict=True)]
                sums += hits
            slots = cell_slots(c)
            out_ref[:, slots] = own_ref[:, slots] - (sums[0] + sums[1] + sums[2])
        return 0

    lax.fori_loop(0, CELLS // 4, four, 0)


def on_device(
    positions, features, tile_first, tile_second, count_first, count_second, w_first, w_second, radial_weight,
    mix_weight, out_weight,
):
    tiles = tile_first.shape[0]
    smem = pl.BlockSpec(memory_space=pltpu.SMEM)
    vmem = pl.BlockSpec(memory_space=pltpu.VMEM)

    anywhere = pl.BlockSpec(memory_space=pl.ANY)
    dma = pltpu.SemaphoreType.DMA
    n = len(WAYS)
    cells = (tiles, CELL, LAT)
    ask, first, second, got_pos = pl.pallas_call(
        functools.partial(fetch_kernel, tiles),
        out_shape=[
            jax.ShapeDtypeStruct((n, tiles, CELL), jnp.int32),
            jax.ShapeDtypeStruct(cells, BF),
            jax.ShapeDtypeStruct(cells, BF),
            jax.ShapeDtypeStruct((n, *positions.shape), BF),
        ],
        in_specs=[smem, smem, anywhere, anywhere],
        out_specs=[vmem, vmem, vmem, anywhere],
        scratch_shapes=[
            pltpu.VMEM((CELLS, CELL, LAT), BF),
            dma(()),
            pltpu.VMEM((tiles, CELL), jnp.int32),
            pltpu.SMEM((n, tiles, CELL), jnp.int32),
        ]
        + [pltpu.VMEM(cells, BF)] * 6
        + [dma((n,))] * 3
        + [dma((GROUPS,))] * 4
        + [dma(())] * 2
        + [dma((n,))] * 2,
        compiler_params=pltpu.CompilerParams(collective_id=0, has_side_effects=True),
        name="fetch",
    )(tile_first, tile_second, positions, features.reshape(-1, CELL, LAT))
    W = ROWS * CELL
    own, partial = pl.pallas_call(
        tile_kernel,
        out_shape=[jax.ShapeDtypeStruct(positions.shape, F32), jax.ShapeDtypeStruct((tiles, 3, CELL), F32)],
        in_specs=[smem] * 4 + [vmem] * 9,
        out_specs=[vmem] * 2,
        scratch_shapes=[
            pltpu.VMEM((tiles, 3, CELL), F32),
            pltpu.VMEM((LAT, LAT), BF),
            pltpu.VMEM((LAT, CELL), F32),
            pltpu.VMEM((tiles, CELL // SUB, 16, LAT), BF),
            pltpu.VMEM((tiles, LAT, CELL), F32),
            pltpu.VMEM((2, tiles + 1, CELL, CELL), F32),
            pltpu.VMEM((tiles, CELL, CELL), F32),
            pltpu.VMEM((tiles, 3, CELL, CELL), F32),
            pltpu.VMEM((LAT, W), F32),
            pltpu.VMEM((LAT, W), F32),
            pltpu.VMEM((LAT, W), F32),
            pltpu.VMEM((LAT, W), F32),
            pltpu.VMEM((NB, W), F32),
        ],
        compiler_params=pltpu.CompilerParams(vmem_limit_bytes=60 << 20),
        name="tiles",
    )(
        tile_first, tile_second, count_first, count_second, positions, got_pos, first, second, w_first, w_second,
        radial_weight, mix_weight, out_weight.reshape(1, LAT),
    )
    return pl.pallas_call(
        functools.partial(return_kernel, tiles),
        out_shape=jax.ShapeDtypeStruct(positions.shape, F32),
        in_specs=[anywhere] * 3,
        out_specs=vmem,
        scratch_shapes=[
            pltpu.VMEM((n, tiles, CELL), jnp.int32),
            pltpu.VMEM(positions.shape, F32),
            pltpu.VMEM((n, tiles, 3, CELL), F32),
            dma((2,)),
            dma((n,)),
            dma((n,)),
        ],
        compiler_params=pltpu.CompilerParams(collective_id=1, has_side_effects=True),
        name="return",
    )(ask, own, partial)


def solution(mesh):
    each = P(("grp", "dev"))
    in_specs = (P(None, ("grp", "dev")), P(("grp", "dev"), None), each, each, each, each, P(), P(), P(), P(), P())
    return jax.shard_map(
        on_device, mesh=mesh, in_specs=in_specs, out_specs=P(None, ("grp", "dev")), check_vma=False
    )
```
